512 devices in a mesh: pairs: 64 (over y, x, core), seg: 8 (over z).
Axes of the slice: x: 4, y: 8, z: 8, core: 2. Of those that a mesh axis runs over, the one named last changes fastest.
Arguments:
- traces: bfloat16 [8, 256, 72000], P('seg', 'pairs')
- block_sources: int32 [64, 26], P('pairs'), may hold values from 0 to 63, as said below
- send_lists: int32 [64, 64, 1], P('pairs'), may hold values from -1 to 3, as said below
Outputs:
- pws: float32 [1600, 3840], P('pairs', 'seg')
The draws below stay inside these ranges and needn't reach their ends.
Inputs may be any that keep to these rules, and one draw needn't show every extreme that they name: `block_sources`: row b names the devices storing block b's 26 stations in order, the virtual source first. No index stands more than 1 times in a row, and in every row some index stands exactly 1 times. send_lists[d, b, j] is the local index, among the 4 stations stored on device d, of the station at the (j + 1)-th position of row b of block_sources that names d, and -1 where d stands fewer than j + 1 times in that row. The stations of one block are distinct.
All inputs are finite; a program needn't handle non-finite values.
Results may differ from the reference program's by a relative error of at most 0.04.
Values may be sent and summed in bfloat16 or wider, within the bound.
No kernel may reach another device: no remote copies, remote signals or barrier semaphores. Data moves between devices by JAX's collectives and lax.ppermute only.
A program may use at most 128 MiB of HBM per device.

```python
import math
import jax
import jax.numpy as jnp
from jax import lax

N1 = 240
N2 = 300
KB = 32
H = 8
STA_DEV = 4
C = 25
L = 72000
NB = 26
BLOCKS = 64
SLOTS = 1
NSTA = 256
SEGS = 8
LAGS = 3840


def routing(key):
    key = jax.random.fold_in(key, 5)
    order_key, offset_key = jax.random.split(key)
    slot_total = BLOCKS * SLOTS
    scores = jax.random.randint(order_key, (BLOCKS, slot_total), 0, 2 ** 20) * slot_total + jnp.arange(slot_total, dtype=jnp.int32)[None, :]
    scores = scores.at[0, (BLOCKS - 1) * SLOTS].set(-2).at[0, 0].set(-1)
    chosen = jnp.argsort(scores, axis=1, stable=True)[:, :NB].astype(jnp.int32)
    sources = chosen // SLOTS
    position = jnp.arange(NB, dtype=jnp.int32)
    earlier = (sources[:, :, None] == sources[:, None, :]) & (position[:, None] > position[None, :])[None]
    repeats = jnp.sum(earlier.astype(jnp.int32), axis=2)
    offsets = jax.random.randint(offset_key, (BLOCKS, BLOCKS), 0, STA_DEV)
    offsets = offsets.at[0, BLOCKS - 1].set(STA_DEV - 1).at[0, 0].set(0)
    station_index = (jnp.take_along_axis(offsets, sources, axis=1) + repeats) % STA_DEV
    devices = jnp.arange(BLOCKS, dtype=jnp.int32)
    slot_ids = jnp.arange(SLOTS, dtype=jnp.int32)
    matched = (sources[None, :, None, :] == devices[:, None, None, None]) & (repeats[None, :, None, :] == slot_ids[None, None, :, None])
    send_table = jnp.max(jnp.where(matched, station_index[None, :, None, :], -1), axis=3)
    return (sources.astype(jnp.int32), send_table.astype(jnp.int32))


def draw_block_sources(key, part):
    shared = routing(key)
    return shared[0]


def draw_send_lists(key, part):
    shared = routing(key)
    return shared[1]


def draw_traces(key, part):
    key = jax.random.fold_in(key, 11)
    noise_key, scale_key, near_key, far_key = jax.random.split(key, 4)
    full_shape = (SEGS, NSTA, L)
    base_noise = jax.random.normal(noise_key, full_shape, jnp.float32)
    loudness = jnp.exp(jax.random.uniform(scale_key, (1, NSTA, 1), jnp.float32, 0.0, math.log(10.0)))
    echo_near = jax.random.uniform(near_key, (1, NSTA, 1), jnp.float32, 0.3, 0.9)
    echo_far = jax.random.uniform(far_key, (1, NSTA, 1), jnp.float32, -0.8, 0.8)
    colored = base_noise + echo_near * jnp.roll(base_noise, 7, axis=2) + echo_far * jnp.roll(base_noise, 23, axis=2)
    return (colored * loudness).astype(jnp.bfloat16)


def setup_inputs(seed: int = 0) -> dict:
    arg_keys = jax.random.split(jax.random.key(seed), 4)
    traces = draw_traces(jax.random.fold_in(arg_keys[3], 71), 0)
    block_sources = draw_block_sources(jax.random.fold_in(arg_keys[3], 71), 0)
    send_lists = draw_send_lists(jax.random.fold_in(arg_keys[3], 71), 0)
    return dict(traces=traces, block_sources=block_sources, send_lists=send_lists)


def angles(left_index, right_index, period):
    product = left_index[:, None] * right_index[None, :] % period
    return product.astype(jnp.float32) * (2.0 * math.pi / period)

def make_tables():
    bins_inner = jnp.arange(N2, dtype=jnp.int32)
    samples_outer = jnp.arange(N1, dtype=jnp.int32)
    band_blocks = jnp.arange(1, KB + 1, dtype=jnp.int32)
    inner_angle = angles(bins_inner, bins_inner, N2)
    inner_table = jnp.concatenate([jnp.cos(inner_angle), -jnp.sin(inner_angle)], 0).astype(jnp.bfloat16)
    twist_angle = angles(bins_inner, samples_outer, N2 * N1)
    twist_cos = jnp.cos(twist_angle).astype(jnp.bfloat16)
    twist_sin = jnp.sin(twist_angle).astype(jnp.bfloat16)
    outer_angle = angles(samples_outer, band_blocks, N1)
    outer_cos = jnp.cos(outer_angle)
    outer_sin = jnp.sin(outer_angle)
    outer_table = jnp.concatenate([jnp.concatenate([outer_cos, -outer_sin], 1), jnp.concatenate([outer_sin, outer_cos], 1)], 0).astype(jnp.bfloat16)
    back_table = jnp.concatenate([jnp.concatenate([outer_cos.T, outer_sin.T], 1), jnp.concatenate([-outer_sin.T, outer_cos.T], 1)], 0).astype(jnp.bfloat16)
    lag_rows = jnp.arange(-H, H, dtype=jnp.int32) % N2
    lag_angle = angles(lag_rows, bins_inner, N2)
    lag_table = jnp.concatenate([jnp.cos(lag_angle), jnp.sin(lag_angle)], 0).astype(jnp.bfloat16)
    return (inner_table, twist_cos, twist_sin, outer_table, back_table, lag_table)

def whiten(spectra):
    real_part = spectra[..., :KB]
    imag_part = spectra[..., KB:]
    magnitude = jnp.sqrt(real_part * real_part + imag_part * imag_part)
    level_mean = lax.optimization_barrier(jnp.mean(magnitude, axis=1, keepdims=True)) + 1e-06
    return (spectra / jnp.concatenate([level_mean, level_mean], -1)).astype(jnp.bfloat16)

def spectrum(records, tables):
    inner_table, twist_cos, twist_sin, outer_table, back_table, lag_table = tables
    number = records.shape[0]
    folded = records.reshape(number, N2, N1).astype(jnp.float32)
    inner_terms = jnp.einsum('kn,tnm->tkm', inner_table.astype(jnp.float32), folded)
    real_part = inner_terms[:, :N2]
    imag_part = inner_terms[:, N2:]
    cosine = twist_cos.astype(jnp.float32)
    sine = twist_sin.astype(jnp.float32)
    turned = jnp.concatenate([real_part * cosine + imag_part * sine, imag_part * cosine - real_part * sine], -1).astype(jnp.bfloat16)
    spectra = jnp.einsum('tkm,mf->tkf', turned.astype(jnp.float32), outer_table.astype(jnp.float32))
    return whiten(spectra)

def lag_partials(source, receivers, tables):
    inner_table, twist_cos, twist_sin, outer_table, back_table, lag_table = tables
    source = source.astype(jnp.float32)
    receivers = receivers.astype(jnp.float32)
    src_real = source[None, :, :KB]
    src_imag = source[None, :, KB:]
    rec_real = receivers[..., :KB]
    rec_imag = receivers[..., KB:]
    correlation = jnp.concatenate([src_real * rec_real + src_imag * rec_imag, src_imag * rec_real - src_real * rec_imag], -1).astype(jnp.bfloat16)
    section_one = jnp.einsum('pkf,fm->pkm', correlation.astype(jnp.float32), back_table.astype(jnp.float32))
    real_part = section_one[..., :N1]
    imag_part = section_one[..., N1:]
    cosine = twist_cos.astype(jnp.float32)
    sine = twist_sin.astype(jnp.float32)
    turned = jnp.concatenate([real_part * cosine - imag_part * sine, real_part * sine + imag_part * cosine], -1).astype(jnp.bfloat16)
    lag_terms = jnp.einsum('jk,pkm->pjm', lag_table.astype(jnp.float32), turned.astype(jnp.float32))
    normalize = 1.0 / math.sqrt(KB * N2)
    real_lag = (lag_terms[:, :2 * H, :N1] - lag_terms[:, 2 * H:, N1:]) * normalize
    imag_lag = (lag_terms[:, 2 * H:, :N1] + lag_terms[:, :2 * H, N1:]) * normalize
    pairs_here = receivers.shape[0]
    real_lag = real_lag.reshape(pairs_here, 2 * H * N1)
    imag_lag = imag_lag.reshape(pairs_here, 2 * H * N1)
    floor_mag = jnp.maximum(jnp.sqrt(real_lag * real_lag + imag_lag * imag_lag), 0.25)
    return jnp.stack([real_lag, real_lag / floor_mag, imag_lag / floor_mag], 0)

def reference(traces, block_sources, send_lists):
    tables = make_tables()
    position = jnp.arange(NB, dtype=jnp.int32)
    earlier = (block_sources[:, :, None] == block_sources[:, None, :]) & (position[:, None] > position[None, :])[None]
    repeats = lax.optimization_barrier(jnp.sum(earlier.astype(jnp.int32), axis=2)).astype(jnp.int32)
    block_ids = jnp.arange(BLOCKS, dtype=jnp.int32)[:, None]
    local_index = send_lists[block_sources, block_ids, repeats]
    station = (block_sources * STA_DEV + local_index).astype(jnp.int32)

    def one_segment(running, segment):
        member_groups = segment.reshape(BLOCKS, STA_DEV, L)
        spectra = lax.map(lambda member_group: spectrum(member_group, tables), member_groups)
        spectra = spectra.reshape(NSTA, N2, 2 * KB)

        def one_block(rows):
            chosen = spectra[rows]
            return lag_partials(chosen[0], chosen[1:], tables)
        return (running + lax.map(one_block, station), None)
    running = jnp.zeros((BLOCKS, 3, C, LAGS), jnp.float32)
    running, unused = lax.scan(one_segment, running, traces)
    linear = running[:, 0] / math.sqrt(SEGS)
    coherence = jnp.sqrt(running[:, 1] * running[:, 1] + running[:, 2] * running[:, 2]) / math.sqrt(SEGS)
    return (linear * coherence).reshape(BLOCKS * C, LAGS)
```

```python
import math

import jax
import jax.numpy as jnp
import numpy as np
from jax import lax
from jax.experimental import pallas as pl
from jax.experimental.pallas import tpu as pltpu
from jax.sharding import PartitionSpec as P

N1 = 240
N2 = 300
KB = 32
H = 8
ROWS = 152
HALF = 64
WIDE = 256
PAIRS = 25
LAGROWS = 56


def angles(left, right, period):
    product = (left[:, None] * right[None, :] % period).astype(np.float32)
    return product * np.float32(2.0 * math.pi / period)


def bf(table):
    return np.asarray(table, np.float32).astype(jnp.bfloat16)


def forward_tables():
    inner = np.arange(N2)
    outer = np.arange(N1)
    band = np.arange(1, KB + 1)
    a = angles(inner, inner, N2)
    dft = np.zeros((4 * ROWS, N2), np.float32)
    dft[:N2] = np.cos(a)
    dft[2 * ROWS : 2 * ROWS + N2] = -np.sin(a)
    t = angles(inner, outer, N1 * N2)
    twist = np.zeros((2, 2 * ROWS, N1), np.float32)
    twist[0, :N2] = np.cos(t)
    twist[1, :N2] = np.sin(t)
    o = angles(outer, band, N1)
    c, s = np.cos(o), np.sin(o)
    last = np.stack([np.concatenate([c, -s, c, -s], 1), np.concatenate([s, c, s, c], 1)])
    return bf(dft), bf(twist), bf(last)


def backward_tables():
    inner = np.arange(N2)
    outer = np.arange(N1)
    band = np.arange(1, KB + 1)
    o = angles(band, outer, N1)
    c, s = np.cos(o), np.sin(o)
    back = np.zeros((4 * HALF, 4 * WIDE), np.float32)
    for h in range(2):
        row, col = h * HALF, 2 * h * WIDE
        re, im = slice(col, col + N1), slice(col + WIDE, col + WIDE + N1)
        for at, to_re, to_im in (
            (row, c, s),
            (row + KB, s, -c),
            (2 * HALF + row, -s, c),
            (2 * HALF + row + KB, c, s),
        ):
            back[at : at + KB, re] = to_re
            back[at : at + KB, im] = to_im
    t = angles(inner, outer, N1 * N2)
    twist = np.zeros((2, 2, ROWS, WIDE), np.float32)
    for h in range(2):
        n = min(ROWS, N2 - h * ROWS)
        twist[h, 0, :n, :N1] = np.cos(t[h * ROWS : h * ROWS + n])
        twist[h, 1, :n, :N1] = np.sin(t[h * ROWS : h * ROWS + n])
    l = angles(np.arange(-H, H) % N2, inner, N2)
    lag = np.zeros((2, 4 * H, ROWS), np.float32)
    for h in range(2):
        n = min(ROWS, N2 - h * ROWS)
        lag[h, : 2 * H, :n] = np.cos(l[:, h * ROWS : h * ROWS + n])
        lag[h, 2 * H :, :n] = np.sin(l[:, h * ROWS : h * ROWS + n])
    return bf(back), bf(twist), bf(lag)


def spectrum_kernel(pick_ref, v_ref, dft_ref, twist_ref, last_ref, out_ref, held):
    cosine = twist_ref[0].astype(jnp.float32)
    sine = twist_ref[1].astype(jnp.float32)
    lane = lax.broadcasted_iota(jnp.int32, (ROWS, 2 * HALF), 1)
    for t in range(v_ref.shape[0]):
        y = jnp.dot(dft_ref[...], v_ref[t], preferred_element_type=jnp.float32)
        re, im = y[: 2 * ROWS], y[2 * ROWS :]
        a = (re * cosine + im * sine).astype(jnp.bfloat16)
        b = (im * cosine - re * sine).astype(jnp.bfloat16)
        x = jnp.dot(a, last_ref[0], preferred_element_type=jnp.float32)
        x = x + jnp.dot(b, last_ref[1], preferred_element_type=jnp.float32)
        power = x * x
        size = jnp.sqrt(power + pltpu.roll(power, KB, 1))
        level = jnp.sum(size, axis=0, keepdims=True) * (1.0 / N2) + 1e-6
        w = x * (1.0 / level)
        held[t] = jnp.where(lane < HALF, w[:ROWS], w[ROWS:]).astype(jnp.bfloat16)

    def send(b, carry):
        out_ref[b] = held[jnp.maximum(pick_ref[b], 0)]
        return carry

    lax.fori_loop(0, out_ref.shape[0], send, 0, unroll=4)


def spectrum_call(pick, v):
    dft, twist, last = forward_tables()
    slots = pick.shape[0]
    vmem = pl.BlockSpec(memory_space=pltpu.VMEM)
    return pl.pallas_call(
        spectrum_kernel,
        out_shape=jax.ShapeDtypeStruct((slots, ROWS, 2 * HALF), jnp.bfloat16),
        in_specs=[pl.BlockSpec(memory_space=pltpu.SMEM), vmem, vmem, vmem, vmem],
        out_specs=vmem,
        scratch_shapes=[pltpu.VMEM((v.shape[0], ROWS, 2 * HALF), jnp.bfloat16)],
        compiler_params=pltpu.CompilerParams(vmem_limit_bytes=48 * 2**20),
        name="spectrum",
    )(pick, v, jnp.asarray(dft), jnp.asarray(twist), jnp.asarray(last))


def lag_kernel(row_ref, w_ref, back_ref, twist_ref, lag_ref, out_ref, stage):
    lane = lax.broadcasted_iota(jnp.int32, (ROWS, 2 * HALF), 1) % HALF
    s = w_ref[row_ref[0]].astype(jnp.float32)
    s1 = jnp.where(lane < KB, s, pltpu.roll(s, KB, 1))
    s2 = jnp.where(lane < KB, pltpu.roll(s, 2 * HALF - KB, 1), s)
    stage[...] = jnp.zeros_like(stage)
    scale = 1.0 / math.sqrt(KB * N2)

    def pair(c, carry):
        r = w_ref[row_ref[c + 1]].astype(jnp.float32)
        both = jnp.concatenate([r * s1, r * s2], 1).astype(jnp.bfloat16)
        total = None
        for h in range(2):
            z = jnp.dot(
                both,
                back_ref[:, 2 * h * WIDE : 2 * (h + 1) * WIDE],
                preferred_element_type=jnp.float32,
            )
            re, im = z[:, :WIDE], z[:, WIDE:]
            cosine = twist_ref[h, 0].astype(jnp.float32)
            sine = twist_ref[h, 1].astype(jnp.float32)
            a = (re * cosine - im * sine).astype(jnp.bfloat16)
            b = (re * sine + im * cosine).astype(jnp.bfloat16)
            ab = jnp.concatenate([a, b], 1)
            part = jnp.dot(lag_ref[h], ab, preferred_element_type=jnp.float32)
            total = part if total is None else total + part
        re = (total[: 2 * H, :WIDE] - total[2 * H :, WIDE:]) * scale
        im = (total[2 * H :, :WIDE] + total[: 2 * H, WIDE:]) * scale
        both = jnp.concatenate([re, im], 1)
        for n in range(2 * H):
            stage[n // 2, pl.ds((n % 2) * PAIRS + c, 1)] = both[n : n + 1]
        return carry

    lax.fori_loop(0, PAIRS, pair, 0)
    out_ref[...] = stage[...].astype(jnp.bfloat16)


def lag_call(rows, w):
    back, twist, lag = backward_tables()
    vmem = pl.BlockSpec(memory_space=pltpu.VMEM)
    return pl.pallas_call(
        lag_kernel,
        out_shape=jax.ShapeDtypeStruct((H, LAGROWS, 2 * WIDE), jnp.bfloat16),
        in_specs=[pl.BlockSpec(memory_space=pltpu.SMEM), vmem, vmem, vmem, vmem],
        out_specs=vmem,
        scratch_shapes=[pltpu.VMEM((H, LAGROWS, 2 * WIDE), jnp.float32)],
        compiler_params=pltpu.CompilerParams(vmem_limit_bytes=48 * 2**20),
        name="lags",
    )(rows, w, jnp.asarray(back), jnp.asarray(twist), jnp.asarray(lag))


def stack_kernel(x_ref, out_ref):
    segments = x_ref.shape[0]
    linear = jnp.zeros((LAGROWS, WIDE), jnp.float32)
    phase_re = jnp.zeros((LAGROWS, WIDE), jnp.float32)
    phase_im = jnp.zeros((LAGROWS, WIDE), jnp.float32)
    for s in range(segments):
        re = x_ref[s, :, :WIDE].astype(jnp.float32)
        im = x_ref[s, :, WIDE:].astype(jnp.float32)
        inverse = 1.0 / jnp.maximum(jnp.sqrt(re * re + im * im), 0.25)
        linear = linear + re
        phase_re = phase_re + re * inverse
        phase_im = phase_im + im * inverse
    coherence = jnp.sqrt(phase_re * phase_re + phase_im * phase_im)
    pws = linear * coherence * (1.0 / segments)
    out_ref[:, :N1] = pws[:PAIRS, :N1]
    out_ref[:, N1:] = pws[PAIRS : 2 * PAIRS, :N1]


def stack_call(x):
    vmem = pl.BlockSpec(memory_space=pltpu.VMEM)
    return pl.pallas_call(
        stack_kernel,
        out_shape=jax.ShapeDtypeStruct((PAIRS, 2 * N1), jnp.float32),
        in_specs=[vmem],
        out_specs=vmem,
        compiler_params=pltpu.CompilerParams(vmem_limit_bytes=48 * 2**20),
        name="stack",
    )(x)


def local(traces, block_sources, send_lists):
    v = traces[0].reshape(traces.shape[1], N2, N1)
    pick = send_lists.reshape(-1)
    rows = block_sources.reshape(-1)
    outgoing = spectrum_call(pick, v)
    arrived = lax.all_to_all(outgoing, "pairs", split_axis=0, concat_axis=0, tiled=True)
    lags = lag_call(rows, arrived)
    lags = lax.all_to_all(lags, "seg", split_axis=0, concat_axis=0, tiled=True)
    return stack_call(lags)


def solution(mesh):
    return jax.shard_map(
        local,
        mesh=mesh,
        in_specs=(P("seg", "pairs", None), P("pairs", None), P("pairs", None, None)),
        out_specs=P("pairs", "seg"),
        check_vma=False,
    )
```

```python
import math

import jax
import jax.numpy as jnp
import numpy as np
from jax import lax
from jax.experimental import pallas as pl
from jax.experimental.pallas import tpu as pltpu
from jax.sharding import PartitionSpec as P

N1 = 240
N2 = 300
KB = 32
H = 8
ROWS = 152
HALF = 64
WIDE = 256
PAIRS = 25
GROUP = 25
LAGROWS = 56


def angles(left, right, period):
    product = (left[:, None] * right[None, :] % period).astype(np.float32)
    return product * np.float32(2.0 * math.pi / period)


def bf(table):
    return np.asarray(table, np.float32).astype(jnp.bfloat16)


def forward_tables():
    inner = np.arange(N2)
    outer = np.arange(N1)
    band = np.arange(1, KB + 1)
    a = angles(inner, inner, N2)
    dft = np.zeros((4 * ROWS, N2), np.float32)
    dft[:N2] = np.cos(a)
    dft[2 * ROWS : 2 * ROWS + N2] = -np.sin(a)
    t = angles(inner, outer, N1 * N2)
    twist = np.zeros((2, 2 * ROWS, N1), np.float32)
    twist[0, :N2] = np.cos(t)
    twist[1, :N2] = np.sin(t)
    o = angles(outer, band, N1)
    c, s = np.cos(o), np.sin(o)
    last = np.stack([np.concatenate([c, -s, c, -s], 1), np.concatenate([s, c, s, c], 1)])
    return bf(dft), bf(twist), bf(last)


def backward_tables():
    inner = np.arange(N2)
    outer = np.arange(N1)
    band = np.arange(1, KB + 1)
    o = angles(band, outer, N1)
    c, s = np.cos(o), np.sin(o)
    back = np.zeros((4 * HALF, 4 * WIDE), np.float32)
    for h in range(2):
        row, col = h * HALF, 2 * h * WIDE
        re, im = slice(col, col + N1), slice(col + WIDE, col + WIDE + N1)
        for at, to_re, to_im in (
            (row, c, s),
            (row + KB, s, -c),
            (2 * HALF + row, -s, c),
            (2 * HALF + row + KB, c, s),
        ):
            back[at : at + KB, re] = to_re
            back[at : at + KB, im] = to_im
    t = angles(inner, outer, N1 * N2)
    twist = np.zeros((2, 2, ROWS, WIDE), np.float32)
    for h in range(2):
        n = min(ROWS, N2 - h * ROWS)
        twist[h, 0, :n, :N1] = np.cos(t[h * ROWS : h * ROWS + n])
        twist[h, 1, :n, :N1] = np.sin(t[h * ROWS : h * ROWS + n])
    l = angles(np.arange(-H, H) % N2, inner, N2)
    lag = np.zeros((2, 4 * H, ROWS), np.float32)
    for h in range(2):
        n = min(ROWS, N2 - h * ROWS)
        lag[h, : 2 * H, :n] = np.cos(l[:, h * ROWS : h * ROWS + n])
        lag[h, 2 * H :, :n] = np.sin(l[:, h * ROWS : h * ROWS + n])
    return bf(back), bf(twist).astype(np.float32), bf(lag)


def spectrum_kernel(
    pick_hbm, v_hbm, dft_hbm, twist_hbm, last_hbm, out_ref, held, pick_ref, v_ref, dft_ref, twist_ref, last_ref, sems
):
    copies = [
        pltpu.make_async_copy(source, target, sems.at[i])
        for i, (source, target) in enumerate(
            (
                (dft_hbm, dft_ref),
                (twist_hbm, twist_ref),
                (last_hbm, last_ref),
                (v_hbm, v_ref),
                (pick_hbm, pick_ref),
            )
        )
    ]
    for copy in copies:
        copy.start()
    for copy in copies:
        copy.wait()
    cosine = twist_ref[0].astype(jnp.float32)
    sine = twist_ref[1].astype(jnp.float32)
    lane = lax.broadcasted_iota(jnp.int32, (ROWS, 2 * HALF), 1)
    for t in range(v_ref.shape[0]):
        y = jnp.dot(dft_ref[...], v_ref[t], preferred_element_type=jnp.float32)
        re, im = y[: 2 * ROWS], y[2 * ROWS :]
        a = (re * cosine + im * sine).astype(jnp.bfloat16)
        b = (im * cosine - re * sine).astype(jnp.bfloat16)
        x = jnp.dot(a, last_ref[0], preferred_element_type=jnp.float32)
        x = x + jnp.dot(b, last_ref[1], preferred_element_type=jnp.float32)
        power = x * x
        size = jnp.sqrt(power + pltpu.roll(power, KB, 1))
        level = jnp.sum(size, axis=0, keepdims=True) * (1.0 / N2) + 1e-6
        w = x * (1.0 / level)
        held[t] = jnp.where(lane < HALF, w[:ROWS], w[ROWS:]).astype(jnp.bfloat16)

    def send(b, carry):
        out_ref[b] = held[jnp.maximum(pick_ref[b], 0)]
        return carry

    lax.fori_loop(0, out_ref.shape[0], send, 0, unroll=4)


def spectrum_call(pick, v):
    dft, twist, last = forward_tables()
    slots = pick.shape[0]
    vmem = pl.BlockSpec(memory_space=pltpu.VMEM)
    hbm = pl.BlockSpec(memory_space=pl.ANY)
    return pl.pallas_call(
        spectrum_kernel,
        out_shape=jax.ShapeDtypeStruct((slots, ROWS, 2 * HALF), jnp.bfloat16),
        in_specs=[hbm, hbm, hbm, hbm, hbm],
        out_specs=vmem,
        scratch_shapes=[
            pltpu.VMEM((v.shape[0], ROWS, 2 * HALF), jnp.bfloat16),
            pltpu.SMEM((slots,), jnp.int32),
            pltpu.VMEM(v.shape, jnp.bfloat16),
            pltpu.VMEM(dft.shape, jnp.bfloat16),
            pltpu.VMEM(twist.shape, jnp.bfloat16),
            pltpu.VMEM(last.shape, jnp.bfloat16),
            pltpu.SemaphoreType.DMA((5,)),
        ],
        compiler_params=pltpu.CompilerParams(vmem_limit_bytes=60 * 2**20),
        name="spectrum",
    )(pick, v, jnp.asarray(dft), jnp.asarray(twist), jnp.asarray(last))


def lag_kernel(row_ref, w_ref, back_ref, twist_ref, lag_ref, out_ref, stage, gather):
    lane = lax.broadcasted_iota(jnp.int32, (ROWS, 2 * HALF), 1) % HALF
    s = w_ref[row_ref[0]].astype(jnp.float32)
    s1 = jnp.where(lane < KB, s, pltpu.roll(s, KB, 1))
    s2 = jnp.where(lane < KB, pltpu.roll(s, 2 * HALF - KB, 1), s)
    scale = 1.0 / math.sqrt(KB * N2)

    def pair(c):
        r = w_ref[row_ref[c + 1]].astype(jnp.float32)
        both = jnp.concatenate([r * s1, r * s2], 1).astype(jnp.bfloat16)
        total = None
        for h in range(2):
            z = jnp.dot(
                both,
                back_ref[:, 2 * h * WIDE : 2 * (h + 1) * WIDE],
                preferred_element_type=jnp.float32,
            )
            re, im = z[:, :WIDE], z[:, WIDE:]
            cosine, sine = twist_ref[h, 0], twist_ref[h, 1]
            a = (re * cosine - im * sine).astype(jnp.bfloat16)
            b = (re * sine + im * cosine).astype(jnp.bfloat16)
            ab = jnp.concatenate([a, b], 1)
            part = jnp.dot(lag_ref[h], ab, preferred_element_type=jnp.float32)
            total = part if total is None else total + part
        re = (total[: 2 * H, :WIDE] - total[2 * H :, WIDE:]) * scale
        im = (total[2 * H :, :WIDE] + total[: 2 * H, WIDE:]) * scale
        at = pl.ds(pl.multiple_of(c * 2 * H, 2 * H), 2 * H)
        for lanes in range(2):
            stage[lanes, at] = re[:, lanes * 128 : (lanes + 1) * 128]
            stage[2 + lanes, at] = im[:, lanes * 128 : (lanes + 1) * 128]

    def group(g, carry):
        for i in range(GROUP):
            pair(g * GROUP + i)
        return carry

    lax.fori_loop(0, PAIRS // GROUP, group, 0)
    gather[...] = jnp.zeros_like(gather)
    for j in range(H):
        for n in range(2):
            for lanes in range(4):
                rows = stage.at[lanes][pl.ds(2 * j + n, PAIRS, stride=2 * H)]
                gather[n * PAIRS : (n + 1) * PAIRS, lanes * 128 : (lanes + 1) * 128] = rows
        out_ref[j] = gather[...].astype(jnp.bfloat16)


def lag_call(rows, w):
    back, twist, lag = backward_tables()
    vmem = pl.BlockSpec(memory_space=pltpu.VMEM)
    return pl.pallas_call(
        lag_kernel,
        out_shape=jax.ShapeDtypeStruct((H, LAGROWS, 2 * WIDE), jnp.bfloat16),
        in_specs=[pl.BlockSpec(memory_space=pltpu.SMEM), vmem, vmem, vmem, vmem],
        out_specs=vmem,
        scratch_shapes=[
            pltpu.VMEM((4, PAIRS * 2 * H, 128), jnp.float32),
            pltpu.VMEM((LAGROWS, 2 * WIDE), jnp.float32),
        ],
        compiler_params=pltpu.CompilerParams(vmem_limit_bytes=48 * 2**20),
        name="lags",
    )(rows, w, jnp.asarray(back), jnp.asarray(twist), jnp.asarray(lag))


def stack_kernel(x_ref, out_ref):
    segments = x_ref.shape[0]
    linear = jnp.zeros((LAGROWS, WIDE), jnp.float32)
    phase_re = jnp.zeros((LAGROWS, WIDE), jnp.float32)
    phase_im = jnp.zeros((LAGROWS, WIDE), jnp.float32)
    for s in range(segments):
        re = x_ref[s, :, :WIDE].astype(jnp.float32)
        im = x_ref[s, :, WIDE:].astype(jnp.float32)
        inverse = 1.0 / jnp.maximum(jnp.sqrt(re * re + im * im), 0.25)
        linear = linear + re
        phase_re = phase_re + re * inverse
        phase_im = phase_im + im * inverse
    coherence = jnp.sqrt(phase_re * phase_re + phase_im * phase_im)
    pws = linear * coherence * (1.0 / segments)
    out_ref[:, :N1] = pws[:PAIRS, :N1]
    out_ref[:, N1:] = pws[PAIRS : 2 * PAIRS, :N1]


def stack_call(x):
    vmem = pl.BlockSpec(memory_space=pltpu.VMEM)
    return pl.pallas_call(
        stack_kernel,
        out_shape=jax.ShapeDtypeStruct((PAIRS, 2 * N1), jnp.float32),
        in_specs=[vmem],
        out_specs=vmem,
        compiler_params=pltpu.CompilerParams(vmem_limit_bytes=48 * 2**20),
        name="stack",
    )(x)


def local(traces, block_sources, send_lists):
    v = traces[0].reshape(traces.shape[1], N2, N1)
    pick = send_lists.reshape(-1)
    rows = block_sources.reshape(-1)
    outgoing = spectrum_call(pick, v)
    arrived = lax.all_to_all(outgoing, "pairs", split_axis=0, concat_axis=0, tiled=True)
    lags = lag_call(rows, arrived)
    lags = lax.all_to_all(lags, "seg", split_axis=0, concat_axis=0, tiled=True)
    return stack_call(lags)


def solution(mesh):
    return jax.shard_map(
        local,
        mesh=mesh,
        in_specs=(P("seg", "pairs", None), P("pairs", None), P("pairs", None, None)),
        out_specs=P("pairs", "seg"),
        check_vma=False,
    )
```

```python
import math

import jax
import jax.numpy as jnp
import numpy as np
from jax import lax
from jax.experimental import pallas as pl
from jax.experimental.pallas import tpu as pltpu
from jax.sharding import Mesh
from jax.sharding import PartitionSpec as P

N1 = 240
N2 = 300
KB = 32
H = 8
ROWS = 152
HALF = 64
WIDE = 256
PAIRS = 25
GROUP = 25
LAGROWS = 56
STATIONS = 4
FAR = 4
NEAR = 16
TAIL = 148


def angles(left, right, period):
    product = (left[:, None] * right[None, :] % period).astype(np.float32)
    return product * np.float32(2.0 * math.pi / period)


def bf(table):
    return np.asarray(table, np.float32).astype(jnp.bfloat16)


def forward_tables():
    inner = np.arange(N2)
    outer = np.arange(N1)
    band = np.arange(1, KB + 1)
    a = angles(inner, inner, N2)
    dft = np.zeros((4 * ROWS, N2), np.float32)
    dft[:N2] = np.cos(a)
    dft[2 * ROWS : 2 * ROWS + N2] = -np.sin(a)
    t = angles(inner, outer, N1 * N2)
    twist = np.zeros((2, 2 * ROWS, N1), np.float32)
    twist[0, :N2] = np.cos(t)
    twist[1, :N2] = np.sin(t)
    o = angles(outer, band, N1)
    c, s = np.cos(o), np.sin(o)
    last = np.stack([np.concatenate([c, -s, c, -s], 1), np.concatenate([s, c, s, c], 1)])
    return bf(dft), bf(twist), bf(last)


def backward_tables():
    inner = np.arange(N2)
    outer = np.arange(N1)
    band = np.arange(1, KB + 1)
    o = angles(band, outer, N1)
    c, s = np.cos(o), np.sin(o)
    back = np.zeros((4 * HALF, 4 * WIDE), np.float32)
    for h in range(2):
        row, col = h * HALF, 2 * h * WIDE
        re, im = slice(col, col + N1), slice(col + WIDE, col + WIDE + N1)
        for at, to_re, to_im in (
            (row, c, s),
            (row + KB, s, -c),
            (2 * HALF + row, -s, c),
            (2 * HALF + row + KB, c, s),
        ):
            back[at : at + KB, re] = to_re
            back[at : at + KB, im] = to_im
    t = angles(inner, outer, N1 * N2)
    twist = np.zeros((2, 2, ROWS, WIDE), np.float32)
    for h in range(2):
        n = min(ROWS, N2 - h * ROWS)
        twist[h, 0, :n, :N1] = np.cos(t[h * ROWS : h * ROWS + n])
        twist[h, 1, :n, :N1] = np.sin(t[h * ROWS : h * ROWS + n])
    l = angles(np.arange(-H, H) % N2, inner, N2)
    lag = np.zeros((2, 4 * H, ROWS), np.float32)
    for h in range(2):
        n = min(ROWS, N2 - h * ROWS)
        lag[h, : 2 * H, :n] = np.cos(l[:, h * ROWS : h * ROWS + n])
        lag[h, 2 * H :, :n] = np.sin(l[:, h * ROWS : h * ROWS + n])
    return bf(back), bf(twist).astype(np.float32), bf(lag)


def spectrum_kernel(
    pick_hbm, v_hbm, dft_hbm, twist_hbm, last_hbm, out_ref, pick_ref, v_ref, dft_ref, twist_ref, last_ref, sems
):
    copies = [
        pltpu.make_async_copy(source, target, sems.at[i])
        for i, (source, target) in enumerate(
            (
                (dft_hbm, dft_ref),
                (twist_hbm, twist_ref),
                (last_hbm, last_ref),
                (v_hbm, v_ref),
                (pick_hbm, pick_ref),
            )
        )
    ]
    for copy in copies:
        copy.start()
    for copy in copies:
        copy.wait()
    cosine = twist_ref[0].astype(jnp.float32)
    sine = twist_ref[1].astype(jnp.float32)
    lane = lax.broadcasted_iota(jnp.int32, (ROWS, 2 * HALF), 1)
    for t in range(v_ref.shape[0]):
        y = jnp.dot(dft_ref[...], v_ref[t], preferred_element_type=jnp.float32)
        re, im = y[: 2 * ROWS], y[2 * ROWS :]
        a = (re * cosine + im * sine).astype(jnp.bfloat16)
        b = (im * cosine - re * sine).astype(jnp.bfloat16)
        x = jnp.dot(a, last_ref[0], preferred_element_type=jnp.float32)
        x = x + jnp.dot(b, last_ref[1], preferred_element_type=jnp.float32)
        power = x * x
        size = jnp.sqrt(power + pltpu.roll(power, KB, 1))
        level = jnp.sum(size, axis=0, keepdims=True) * (1.0 / N2) + 1e-6
        w = x * (1.0 / level)
        packed = jnp.where(lane < HALF, w[:ROWS], w[ROWS:])
        row = lax.broadcasted_iota(jnp.int32, (8, 2 * HALF), 0) + (ROWS - 8)
        upper = lax.broadcasted_iota(jnp.int32, (8, 2 * HALF), 1) >= HALF
        for f in range(FAR):
            tail = packed[ROWS - 8 :]
            for i in range(NEAR // STATIONS):
                wanted = pick_ref[f * NEAR + t * (NEAR // STATIONS) + i].astype(jnp.float32)
                tail = jnp.where((row == TAIL + i) & upper, wanted, tail)
            out_ref[f, t] = jnp.concatenate([packed[: ROWS - 8], tail], 0).astype(jnp.bfloat16)


def spectrum_call(pick, v):
    dft, twist, last = forward_tables()
    vmem = pl.BlockSpec(memory_space=pltpu.VMEM)
    hbm = pl.BlockSpec(memory_space=pl.ANY)
    return pl.pallas_call(
        spectrum_kernel,
        out_shape=jax.ShapeDtypeStruct((FAR, STATIONS, ROWS, 2 * HALF), jnp.bfloat16),
        in_specs=[hbm, hbm, hbm, hbm, hbm],
        out_specs=vmem,
        scratch_shapes=[
            pltpu.SMEM(pick.shape, jnp.int32),
            pltpu.VMEM(v.shape, jnp.bfloat16),
            pltpu.VMEM(dft.shape, jnp.bfloat16),
            pltpu.VMEM(twist.shape, jnp.bfloat16),
            pltpu.VMEM(last.shape, jnp.bfloat16),
            pltpu.SemaphoreType.DMA((5,)),
        ],
        compiler_params=pltpu.CompilerParams(vmem_limit_bytes=60 * 2**20),
        name="spectrum",
    )(pick, v, jnp.asarray(dft), jnp.asarray(twist), jnp.asarray(last))


def choose_kernel(x_ref, out_ref):
    lane = lax.broadcasted_iota(jnp.int32, (8, 2 * HALF), 1)
    for f in range(FAR):
        for d in range(NEAR):
            tail = x_ref[f, d // 4, ROWS - 16 :].astype(jnp.float32)[8:]
            wanted = jnp.where(lane < HALF, pltpu.roll(tail, HALF, 1), tail)
            wanted = wanted[TAIL - ROWS + 8 + d % 4 :][:1]
            total = None
            for t in range(STATIONS):
                mask = jnp.where(wanted == t, 1.0, 0.0)
                mask = jnp.broadcast_to(mask, (16, 2 * HALF)).astype(jnp.bfloat16)
                mask = jnp.concatenate([mask] * 10, 0)[:ROWS]
                part = x_ref[f, t] * mask
                total = part if total is None else total + part
            out_ref[d, f] = total


def choose_call(x):
    vmem = pl.BlockSpec(memory_space=pltpu.VMEM)
    return pl.pallas_call(
        choose_kernel,
        out_shape=jax.ShapeDtypeStruct((NEAR, FAR, ROWS, 2 * HALF), jnp.bfloat16),
        in_specs=[vmem],
        out_specs=vmem,
        compiler_params=pltpu.CompilerParams(vmem_limit_bytes=48 * 2**20),
        name="choose",
    )(x)


def place(owner):
    return (owner & (NEAR - 1)) * FAR + (owner >> 4)


def lag_kernel(row_ref, w_ref, back_ref, twist_ref, lag_ref, out_ref, stage, gather):
    lane = lax.broadcasted_iota(jnp.int32, (ROWS, 2 * HALF), 1) % HALF
    s = w_ref[place(row_ref[0])].astype(jnp.float32)
    s1 = jnp.where(lane < KB, s, pltpu.roll(s, KB, 1))
    s2 = jnp.where(lane < KB, pltpu.roll(s, 2 * HALF - KB, 1), s)
    scale = 1.0 / math.sqrt(KB * N2)

    def pair(c):
        r = w_ref[place(row_ref[c + 1])].astype(jnp.float32)
        both = jnp.concatenate([r * s1, r * s2], 1).astype(jnp.bfloat16)
        total = None
        for h in range(2):
            z = jnp.dot(
                both,
                back_ref[:, 2 * h * WIDE : 2 * (h + 1) * WIDE],
                preferred_element_type=jnp.float32,
            )
            re, im = z[:, :WIDE], z[:, WIDE:]
            cosine, sine = twist_ref[h, 0], twist_ref[h, 1]
            a = (re * cosine - im * sine).astype(jnp.bfloat16)
            b = (re * sine + im * cosine).astype(jnp.bfloat16)
            ab = jnp.concatenate([a, b], 1)
            part = jnp.dot(lag_ref[h], ab, preferred_element_type=jnp.float32)
            total = part if total is None else total + part
        re = (total[: 2 * H, :WIDE] - total[2 * H :, WIDE:]) * scale
        im = (total[2 * H :, :WIDE] + total[: 2 * H, WIDE:]) * scale
        at = pl.ds(pl.multiple_of(c * 2 * H, 2 * H), 2 * H)
        for lanes in range(2):
            stage[lanes, at] = re[:, lanes * 128 : (lanes + 1) * 128]
            stage[2 + lanes, at] = im[:, lanes * 128 : (lanes + 1) * 128]

    def group(g, carry):
        for i in range(GROUP):
            pair(g * GROUP + i)
        return carry

    lax.fori_loop(0, PAIRS // GROUP, group, 0)
    gather[...] = jnp.zeros_like(gather)
    for j in range(H):
        for n in range(2):
            for lanes in range(4):
                rows = stage.at[lanes][pl.ds(2 * j + n, PAIRS, stride=2 * H)]
                gather[n * PAIRS : (n + 1) * PAIRS, lanes * 128 : (lanes + 1) * 128] = rows
        out_ref[j] = gather[...].astype(jnp.bfloat16)


def lag_call(rows, w):
    back, twist, lag = backward_tables()
    vmem = pl.BlockSpec(memory_space=pltpu.VMEM)
    return pl.pallas_call(
        lag_kernel,
        out_shape=jax.ShapeDtypeStruct((H, LAGROWS, 2 * WIDE), jnp.bfloat16),
        in_specs=[pl.BlockSpec(memory_space=pltpu.SMEM), vmem, vmem, vmem, vmem],
        out_specs=vmem,
        scratch_shapes=[
            pltpu.VMEM((4, PAIRS * 2 * H, 128), jnp.float32),
            pltpu.VMEM((LAGROWS, 2 * WIDE), jnp.float32),
        ],
        compiler_params=pltpu.CompilerParams(vmem_limit_bytes=48 * 2**20),
        name="lags",
    )(rows, w, jnp.asarray(back), jnp.asarray(twist), jnp.asarray(lag))


def stack_kernel(x_ref, out_ref):
    segments = x_ref.shape[0]
    linear = jnp.zeros((LAGROWS, WIDE), jnp.float32)
    phase_re = jnp.zeros((LAGROWS, WIDE), jnp.float32)
    phase_im = jnp.zeros((LAGROWS, WIDE), jnp.float32)
    for s in range(segments):
        re = x_ref[s, :, :WIDE].astype(jnp.float32)
        im = x_ref[s, :, WIDE:].astype(jnp.float32)
        inverse = 1.0 / jnp.maximum(jnp.sqrt(re * re + im * im), 0.25)
        linear = linear + re
        phase_re = phase_re + re * inverse
        phase_im = phase_im + im * inverse
    coherence = jnp.sqrt(phase_re * phase_re + phase_im * phase_im)
    pws = linear * coherence * (1.0 / segments)
    out_ref[:, :N1] = pws[:PAIRS, :N1]
    out_ref[:, N1:] = pws[PAIRS : 2 * PAIRS, :N1]


def stack_call(x):
    vmem = pl.BlockSpec(memory_space=pltpu.VMEM)
    return pl.pallas_call(
        stack_kernel,
        out_shape=jax.ShapeDtypeStruct((PAIRS, 2 * N1), jnp.float32),
        in_specs=[vmem],
        out_specs=vmem,
        compiler_params=pltpu.CompilerParams(vmem_limit_bytes=48 * 2**20),
        name="stack",
    )(x)


def local(traces, block_sources, send_lists):
    v = traces[0].reshape(STATIONS, N2, N1)
    pick = send_lists.reshape(-1)
    rows = block_sources.reshape(-1)
    whitened = spectrum_call(pick, v)
    whitened = lax.all_to_all(whitened, "far", split_axis=0, concat_axis=0, tiled=True)
    chosen = choose_call(whitened)
    chosen = lax.all_to_all(chosen, ("near", "cell"), split_axis=0, concat_axis=0, tiled=True)
    lags = lag_call(rows, chosen.reshape(FAR * NEAR, ROWS, 2 * HALF))
    lags = lax.all_to_all(lags, "seg", split_axis=0, concat_axis=0, tiled=True)
    return stack_call(lags)


def solution(mesh):
    split = Mesh(mesh.devices.reshape(FAR, 2, NEAR // 2, -1), ("far", "near", "cell", "seg"))
    pairs = ("far", "near", "cell")
    return jax.shard_map(
        local,
        mesh=split,
        in_specs=(P("seg", pairs, None), P(pairs, None), P(pairs, None, None)),
        out_specs=P(pairs, "seg"),
        check_vma=False,
    )
```

```python
import math

import jax
import jax.numpy as jnp
import numpy as np
from jax import lax
from jax.experimental import pallas as pl
from jax.experimental.pallas import tpu as pltpu
from jax.sharding import Mesh
from jax.sharding import PartitionSpec as P

N1 = 240
N2 = 300
KB = 32
H = 8
ROWS = 152
HALF = 64
WIDE = 256
PAIRS = 25
GROUP = 25
LAGROWS = 56
STATIONS = 4
FAR = 4
NEAR = 16
FOLD = 8
STEP = FOLD * N1
FULL = N2 // FOLD
STAGED = 40
TAIL = 148


def angles(left, right, period):
    product = (left[:, None] * right[None, :] % period).astype(np.float32)
    return product * np.float32(2.0 * math.pi / period)


def bf(table):
    return np.asarray(table, np.float32).astype(jnp.bfloat16)


def forward_tables():
    inner = np.arange(N2)
    outer = np.arange(N1)
    band = np.arange(1, KB + 1)
    a = angles(inner, inner, N2)
    dft = np.zeros((4 * ROWS, FOLD * STAGED), np.float32)
    column = inner % FOLD * STAGED + inner // FOLD
    dft[:N2, column] = np.cos(a)
    dft[2 * ROWS : 2 * ROWS + N2, column] = -np.sin(a)
    t = angles(inner, outer, N1 * N2)
    twist = np.zeros((2, 2 * ROWS, N1), np.float32)
    twist[0, :N2] = np.cos(t)
    twist[1, :N2] = np.sin(t)
    o = angles(outer, band, N1)
    c, s = np.cos(o), np.sin(o)
    last = np.stack([np.concatenate([c, -s, c, -s], 1), np.concatenate([s, c, s, c], 1)])
    return bf(dft), bf(twist), bf(last)


def backward_tables():
    inner = np.arange(N2)
    outer = np.arange(N1)
    band = np.arange(1, KB + 1)
    o = angles(band, outer, N1)
    c, s = np.cos(o), np.sin(o)
    back = np.zeros((4 * HALF, 4 * WIDE), np.float32)
    for h in range(2):
        row, col = h * HALF, 2 * h * WIDE
        re, im = slice(col, col + N1), slice(col + WIDE, col + WIDE + N1)
        for at, to_re, to_im in (
            (row, c, s),
            (row + KB, s, -c),
            (2 * HALF + row, -s, c),
            (2 * HALF + row + KB, c, s),
        ):
            back[at : at + KB, re] = to_re
            back[at : at + KB, im] = to_im
    t = angles(inner, outer, N1 * N2)
    twist = np.zeros((2, 2, ROWS, WIDE), np.float32)
    for h in range(2):
        n = min(ROWS, N2 - h * ROWS)
        twist[h, 0, :n, :N1] = np.cos(t[h * ROWS : h * ROWS + n])
        twist[h, 1, :n, :N1] = np.sin(t[h * ROWS : h * ROWS + n])
    l = angles(np.arange(-H, H) % N2, inner, N2)
    lag = np.zeros((2, 4 * H, ROWS), np.float32)
    for h in range(2):
        n = min(ROWS, N2 - h * ROWS)
        lag[h, : 2 * H, :n] = np.cos(l[:, h * ROWS : h * ROWS + n])
        lag[h, 2 * H :, :n] = np.sin(l[:, h * ROWS : h * ROWS + n])
    return bf(back), bf(twist), bf(np.concatenate([lag[0], lag[1]], 1))


def spectrum_kernel(
    pick_hbm, x_hbm, dft_hbm, twist_hbm, last_hbm, out_ref, pick_ref, x_ref, stage, dft_ref, twist_ref, last_ref, sems
):
    copies = [
        pltpu.make_async_copy(source, target, sems.at[i])
        for i, (source, target) in enumerate(
            (
                (x_hbm, x_ref),
                (dft_hbm, dft_ref),
                (twist_hbm, twist_ref),
                (last_hbm, last_ref),
                (pick_hbm, pick_ref),
            )
        )
    ]
    for copy in copies:
        copy.start()
    tiles = STEP // 128
    copies[0].wait()
    stage[:, STAGED * STATIONS - 16 :] = jnp.zeros((tiles, 16, 128), jnp.float32)
    for a in range(FULL):
        chunk = x_ref[0, :, a * STEP : (a + 1) * STEP].astype(jnp.float32)
        for c in range(tiles):
            stage[c, a * STATIONS : (a + 1) * STATIONS] = chunk[:, c * 128 : (c + 1) * 128]
    rest = x_ref[0, :, FULL * STEP :].astype(jnp.float32)
    rest = jnp.concatenate([rest, jnp.zeros((STATIONS, STEP - rest.shape[1]), jnp.float32)], 1)
    for c in range(tiles):
        stage[c, FULL * STATIONS : (FULL + 1) * STATIONS] = rest[:, c * 128 : (c + 1) * 128]
    for copy in copies[1:]:
        copy.wait()
    cosine = twist_ref[0].astype(jnp.float32)
    sine = twist_ref[1].astype(jnp.float32)
    lane = lax.broadcasted_iota(jnp.int32, (ROWS, 2 * HALF), 1)
    for t in range(STATIONS):
        at = pl.ds(t, STAGED, stride=STATIONS)
        rows = jnp.concatenate([stage.at[c][at] for c in range(tiles)], 1)
        v = jnp.concatenate([rows[:, r * N1 : (r + 1) * N1] for r in range(FOLD)], 0)
        y = jnp.dot(dft_ref[...], v.astype(jnp.bfloat16), preferred_element_type=jnp.float32)
        re, im = y[: 2 * ROWS], y[2 * ROWS :]
        a = (re * cosine + im * sine).astype(jnp.bfloat16)
        b = (im * cosine - re * sine).astype(jnp.bfloat16)
        x = jnp.dot(a, last_ref[0], preferred_element_type=jnp.float32)
        x = x + jnp.dot(b, last_ref[1], preferred_element_type=jnp.float32)
        power = x * x
        size = jnp.sqrt(power + pltpu.roll(power, KB, 1))
        level = jnp.sum(size, axis=0, keepdims=True) * (1.0 / N2) + 1e-6
        w = x * (1.0 / level)
        packed = jnp.where(lane < HALF, w[:ROWS], w[ROWS:])
        row = lax.broadcasted_iota(jnp.int32, (8, 2 * HALF), 0) + (ROWS - 8)
        upper = lax.broadcasted_iota(jnp.int32, (8, 2 * HALF), 1) >= HALF
        for f in range(FAR):
            tail = packed[ROWS - 8 :]
            for i in range(NEAR // STATIONS):
                wanted = pick_ref[f * NEAR + t * (NEAR // STATIONS) + i].astype(jnp.float32)
                tail = jnp.where((row == TAIL + i) & upper, wanted, tail)
            out_ref[f, t] = jnp.concatenate([packed[: ROWS - 8], tail], 0).astype(jnp.bfloat16)


def spectrum_call(pick, x):
    dft, twist, last = forward_tables()
    vmem = pl.BlockSpec(memory_space=pltpu.VMEM)
    hbm = pl.BlockSpec(memory_space=pl.ANY)
    return pl.pallas_call(
        spectrum_kernel,
        out_shape=jax.ShapeDtypeStruct((FAR, STATIONS, ROWS, 2 * HALF), jnp.bfloat16),
        in_specs=[hbm, hbm, hbm, hbm, hbm],
        out_specs=vmem,
        scratch_shapes=[
            pltpu.SMEM(pick.shape, jnp.int32),
            pltpu.VMEM(x.shape, jnp.bfloat16),
            pltpu.VMEM((STEP // 128, STAGED * STATIONS, 128), jnp.float32),
            pltpu.VMEM(dft.shape, jnp.bfloat16),
            pltpu.VMEM(twist.shape, jnp.bfloat16),
            pltpu.VMEM(last.shape, jnp.bfloat16),
            pltpu.SemaphoreType.DMA((5,)),
        ],
        compiler_params=pltpu.CompilerParams(vmem_limit_bytes=60 * 2**20),
        name="spectrum",
    )(pick, x, jnp.asarray(dft), jnp.asarray(twist), jnp.asarray(last))


def choose_kernel(x_ref, out_ref):
    lane = lax.broadcasted_iota(jnp.int32, (8, 2 * HALF), 1)
    for f in range(FAR):
        for d in range(NEAR):
            tail = x_ref[f, d // 4, ROWS - 16 :].astype(jnp.float32)[8:]
            wanted = jnp.where(lane < HALF, pltpu.roll(tail, HALF, 1), tail)
            wanted = wanted[TAIL - ROWS + 8 + d % 4 :][:1]
            total = None
            for t in range(STATIONS):
                mask = jnp.where(wanted == t, 1.0, 0.0)
                mask = jnp.broadcast_to(mask, (16, 2 * HALF)).astype(jnp.bfloat16)
                mask = jnp.concatenate([mask] * 10, 0)[:ROWS]
                part = x_ref[f, t] * mask
                total = part if total is None else total + part
            out_ref[d, f] = total


def choose_call(x):
    vmem = pl.BlockSpec(memory_space=pltpu.VMEM)
    return pl.pallas_call(
        choose_kernel,
        out_shape=jax.ShapeDtypeStruct((NEAR, FAR, ROWS, 2 * HALF), jnp.bfloat16),
        in_specs=[vmem],
        out_specs=vmem,
        compiler_params=pltpu.CompilerParams(vmem_limit_bytes=48 * 2**20),
        name="choose",
    )(x)


def place(owner):
    return (owner & (NEAR - 1)) * FAR + (owner >> 4)


def lag_kernel(row_ref, w_ref, back_ref, twist_ref, lag_ref, out_ref, stage, gather):
    lane = lax.broadcasted_iota(jnp.int32, (ROWS, 2 * HALF), 1) % HALF
    s = w_ref[place(row_ref[0])].astype(jnp.float32)
    s1 = jnp.where(lane < KB, s, pltpu.roll(s, KB, 1)).astype(jnp.bfloat16)
    s2 = jnp.where(lane < KB, pltpu.roll(s, 2 * HALF - KB, 1), s).astype(jnp.bfloat16)
    scale = 1.0 / math.sqrt(KB * N2)

    def pair(c):
        r = w_ref[place(row_ref[c + 1])]
        both = jnp.concatenate([r * s1, r * s2], 1)
        halves = []
        for h in range(2):
            z = jnp.dot(
                both,
                back_ref[:, 2 * h * WIDE : 2 * (h + 1) * WIDE],
                preferred_element_type=jnp.float32,
            )
            re, im = z[:, :WIDE].astype(jnp.bfloat16), z[:, WIDE:].astype(jnp.bfloat16)
            cosine, sine = twist_ref[h, 0], twist_ref[h, 1]
            a = re * cosine - im * sine
            b = re * sine + im * cosine
            ab = jnp.concatenate([a, b], 1)
            halves.append(ab)
        total = jnp.dot(lag_ref[...], jnp.concatenate(halves, 0), preferred_element_type=jnp.float32)
        re = (total[: 2 * H, :WIDE] - total[2 * H :, WIDE:]) * scale
        im = (total[2 * H :, :WIDE] + total[: 2 * H, WIDE:]) * scale
        at = pl.ds(pl.multiple_of(c * 2 * H, 2 * H), 2 * H)
        for lanes in range(2):
            stage[lanes, at] = re[:, lanes * 128 : (lanes + 1) * 128]
            stage[2 + lanes, at] = im[:, lanes * 128 : (lanes + 1) * 128]

    def group(g, carry):
        for i in range(GROUP):
            pair(g * GROUP + i)
        return carry

    lax.fori_loop(0, PAIRS // GROUP, group, 0)
    gather[...] = jnp.zeros_like(gather)
    for j in range(H):
        for n in range(2):
            for lanes in range(4):
                rows = stage.at[lanes][pl.ds(2 * j + n, PAIRS, stride=2 * H)]
                gather[n * PAIRS : (n + 1) * PAIRS, lanes * 128 : (lanes + 1) * 128] = rows
        out_ref[j] = gather[...].astype(jnp.bfloat16)


def lag_call(rows, w):
    back, twist, lag = backward_tables()
    vmem = pl.BlockSpec(memory_space=pltpu.VMEM)
    return pl.pallas_call(
        lag_kernel,
        out_shape=jax.ShapeDtypeStruct((H, LAGROWS, 2 * WIDE), jnp.bfloat16),
        in_specs=[pl.BlockSpec(memory_space=pltpu.SMEM), vmem, vmem, vmem, vmem],
        out_specs=vmem,
        scratch_shapes=[
            pltpu.VMEM((4, PAIRS * 2 * H, 128), jnp.float32),
            pltpu.VMEM((LAGROWS, 2 * WIDE), jnp.float32),
        ],
        compiler_params=pltpu.CompilerParams(vmem_limit_bytes=48 * 2**20),
        name="lags",
    )(rows, w, jnp.asarray(back), jnp.asarray(twist), jnp.asarray(lag))


def stack_kernel(x_ref, out_ref):
    segments = x_ref.shape[0]
    linear = jnp.zeros((LAGROWS, WIDE), jnp.float32)
    phase_re = jnp.zeros((LAGROWS, WIDE), jnp.float32)
    phase_im = jnp.zeros((LAGROWS, WIDE), jnp.float32)
    for s in range(segments):
        re = x_ref[s, :, :WIDE].astype(jnp.float32)
        im = x_ref[s, :, WIDE:].astype(jnp.float32)
        inverse = 1.0 / jnp.maximum(jnp.sqrt(re * re + im * im), 0.25)
        linear = linear + re
        phase_re = phase_re + re * inverse
        phase_im = phase_im + im * inverse
    coherence = jnp.sqrt(phase_re * phase_re + phase_im * phase_im)
    pws = linear * coherence * (1.0 / segments)
    out_ref[:, :N1] = pws[:PAIRS, :N1]
    out_ref[:, N1:] = pws[PAIRS : 2 * PAIRS, :N1]


def stack_call(x):
    vmem = pl.BlockSpec(memory_space=pltpu.VMEM)
    return pl.pallas_call(
        stack_kernel,
        out_shape=jax.ShapeDtypeStruct((PAIRS, 2 * N1), jnp.float32),
        in_specs=[vmem],
        out_specs=vmem,
        compiler_params=pltpu.CompilerParams(vmem_limit_bytes=48 * 2**20),
        name="stack",
    )(x)


def local(traces, block_sources, send_lists):
    pick = send_lists.reshape(-1)
    rows = block_sources.reshape(-1)
    whitened = spectrum_call(pick, traces)
    whitened = lax.all_to_all(whitened, "far", split_axis=0, concat_axis=0, tiled=True)
    chosen = choose_call(whitened)
    chosen = lax.all_to_all(chosen, ("near", "cell"), split_axis=0, concat_axis=0, tiled=True)
    lags = lag_call(rows, chosen.reshape(FAR * NEAR, ROWS, 2 * HALF))
    lags = lax.all_to_all(lags, "seg", split_axis=0, concat_axis=0, tiled=True)
    return stack_call(lags)


def solution(mesh):
    split = Mesh(mesh.devices.reshape(FAR, 2, NEAR // 2, -1), ("far", "near", "cell", "seg"))
    pairs = ("far", "near", "cell")
    return jax.shard_map(
        local,
        mesh=split,
        in_specs=(P("seg", pairs, None), P(pairs, None), P(pairs, None, None)),
        out_specs=P(pairs, "seg"),
        check_vma=False,
    )
```

```python
import math

import jax
import jax.numpy as jnp
import numpy as np
from jax import lax
from jax.experimental import pallas as pl
from jax.experimental.pallas import tpu as pltpu
from jax.sharding import Mesh
from jax.sharding import PartitionSpec as P

N1 = 240
N2 = 300
KB = 32
H = 8
ROWS = 152
HALF = 64
WIDE = 256
PAIRS = 25
PITCH = 160
LAGROWS = 56
STATIONS = 4
FAR = 4
NEAR = 16
FOLD = 8
STEP = FOLD * N1
FULL = N2 // FOLD
STAGED = 40
TAIL = 148


def angles(left, right, period):
    product = (left[:, None] * right[None, :] % period).astype(np.float32)
    return product * np.float32(2.0 * math.pi / period)


def bf(table):
    return np.asarray(table, np.float32).astype(jnp.bfloat16)


def forward_tables():
    inner = np.arange(N2)
    outer = np.arange(N1)
    band = np.arange(1, KB + 1)
    a = angles(inner, inner, N2)
    dft = np.zeros((4 * ROWS, FOLD * STAGED), np.float32)
    column = inner % FOLD * STAGED + inner // FOLD
    dft[:N2, column] = np.cos(a)
    dft[2 * ROWS : 2 * ROWS + N2, column] = -np.sin(a)
    t = angles(inner, outer, N1 * N2)
    twist = np.zeros((2, 2 * ROWS, N1), np.float32)
    twist[0, :N2] = np.cos(t)
    twist[1, :N2] = np.sin(t)
    o = angles(outer, band, N1)
    c, s = np.cos(o), np.sin(o)
    last = np.stack([np.concatenate([c, -s, c, -s], 1), np.concatenate([s, c, s, c], 1)])
    return bf(dft), bf(twist), bf(last)


def backward_tables():
    inner = np.arange(N2)
    outer = np.arange(N1)
    band = np.arange(1, KB + 1)
    o = angles(band, outer, N1)
    c, s = np.cos(o), np.sin(o)
    back = np.zeros((4 * HALF, 4 * WIDE), np.float32)
    for h in range(2):
        row, col = h * HALF, 2 * h * WIDE
        re, im = slice(col, col + N1), slice(col + WIDE, col + WIDE + N1)
        for at, to_re, to_im in (
            (row, c, s),
            (row + KB, s, -c),
            (2 * HALF + row, -s, c),
            (2 * HALF + row + KB, c, s),
        ):
            back[at : at + KB, re] = to_re
            back[at : at + KB, im] = to_im
    t = angles(inner, outer, N1 * N2)
    twist = np.zeros((2, 2, ROWS, WIDE), np.float32)
    for h in range(2):
        n = min(ROWS, N2 - h * ROWS)
        twist[h, 0, :n, :N1] = np.cos(t[h * ROWS : h * ROWS + n])
        twist[h, 1, :n, :N1] = np.sin(t[h * ROWS : h * ROWS + n])
    l = angles(np.arange(-H, H) % N2, inner, N2)
    lag = np.zeros((2, 4 * H, ROWS), np.float32)
    for h in range(2):
        n = min(ROWS, N2 - h * ROWS)
        lag[h, : 2 * H, :n] = np.cos(l[:, h * ROWS : h * ROWS + n])
        lag[h, 2 * H :, :n] = np.sin(l[:, h * ROWS : h * ROWS + n])
    return bf(back), bf(twist), bf(np.concatenate([lag[0], lag[1]], 1))


def spectrum_kernel(
    pick_hbm, x_hbm, dft_hbm, twist_hbm, last_hbm, out_ref, pick_ref, x_ref, stage, dft_ref, twist_ref, last_ref, sems
):
    copies = [
        pltpu.make_async_copy(source, target, sems.at[i])
        for i, (source, target) in enumerate(
            (
                (x_hbm, x_ref),
                (dft_hbm, dft_ref),
                (twist_hbm, twist_ref),
                (last_hbm, last_ref),
                (pick_hbm, pick_ref),
            )
        )
    ]
    for copy in copies:
        copy.start()
    tiles = STEP // 128
    copies[0].wait()
    stage[:, STAGED * STATIONS - 16 :] = jnp.zeros((tiles, 16, 128), jnp.float32)
    for a in range(FULL):
        chunk = x_ref[0, :, a * STEP : (a + 1) * STEP].astype(jnp.float32)
        for c in range(tiles):
            stage[c, a * STATIONS : (a + 1) * STATIONS] = chunk[:, c * 128 : (c + 1) * 128]
    rest = x_ref[0, :, FULL * STEP :].astype(jnp.float32)
    rest = jnp.concatenate([rest, jnp.zeros((STATIONS, STEP - rest.shape[1]), jnp.float32)], 1)
    for c in range(tiles):
        stage[c, FULL * STATIONS : (FULL + 1) * STATIONS] = rest[:, c * 128 : (c + 1) * 128]
    for copy in copies[1:]:
        copy.wait()
    cosine = twist_ref[0].astype(jnp.float32)
    sine = twist_ref[1].astype(jnp.float32)
    lane = lax.broadcasted_iota(jnp.int32, (ROWS, 2 * HALF), 1)
    for t in range(STATIONS):
        at = pl.ds(t, STAGED, stride=STATIONS)
        rows = jnp.concatenate([stage.at[c][at] for c in range(tiles)], 1)
        v = jnp.concatenate([rows[:, r * N1 : (r + 1) * N1] for r in range(FOLD)], 0)
        y = jnp.dot(dft_ref[...], v.astype(jnp.bfloat16), preferred_element_type=jnp.float32)
        re, im = y[: 2 * ROWS], y[2 * ROWS :]
        a = (re * cosine + im * sine).astype(jnp.bfloat16)
        b = (im * cosine - re * sine).astype(jnp.bfloat16)
        x = jnp.dot(a, last_ref[0], preferred_element_type=jnp.float32)
        x = x + jnp.dot(b, last_ref[1], preferred_element_type=jnp.float32)
        power = x * x
        size = jnp.sqrt(power + pltpu.roll(power, KB, 1))
        level = jnp.sum(size, axis=0, keepdims=True) * (1.0 / N2) + 1e-6
        w = x * (1.0 / level)
        packed = jnp.where(lane < HALF, w[:ROWS], w[ROWS:])
        row = lax.broadcasted_iota(jnp.int32, (8, 2 * HALF), 0) + (ROWS - 8)
        upper = lax.broadcasted_iota(jnp.int32, (8, 2 * HALF), 1) >= HALF
        for f in range(FAR):
            tail = packed[ROWS - 8 :]
            for i in range(NEAR // STATIONS):
                wanted = pick_ref[f * NEAR + t * (NEAR // STATIONS) + i].astype(jnp.float32)
                tail = jnp.where((row == TAIL + i) & upper, wanted, tail)
            out_ref[f, t] = jnp.concatenate([packed[: ROWS - 8], tail], 0).astype(jnp.bfloat16)


def spectrum_call(pick, x):
    dft, twist, last = forward_tables()
    vmem = pl.BlockSpec(memory_space=pltpu.VMEM)
    hbm = pl.BlockSpec(memory_space=pl.ANY)
    return pl.pallas_call(
        spectrum_kernel,
        out_shape=jax.ShapeDtypeStruct((FAR, STATIONS, ROWS, 2 * HALF), jnp.bfloat16),
        in_specs=[hbm, hbm, hbm, hbm, hbm],
        out_specs=vmem,
        scratch_shapes=[
            pltpu.SMEM(pick.shape, jnp.int32),
            pltpu.VMEM(x.shape, jnp.bfloat16),
            pltpu.VMEM((STEP // 128, STAGED * STATIONS, 128), jnp.float32),
            pltpu.VMEM(dft.shape, jnp.bfloat16),
            pltpu.VMEM(twist.shape, jnp.bfloat16),
            pltpu.VMEM(last.shape, jnp.bfloat16),
            pltpu.SemaphoreType.DMA((5,)),
        ],
        compiler_params=pltpu.CompilerParams(vmem_limit_bytes=60 * 2**20),
        name="spectrum",
    )(pick, x, jnp.asarray(dft), jnp.asarray(twist), jnp.asarray(last))


def choose_kernel(x_ref, out_ref):
    lane = lax.broadcasted_iota(jnp.int32, (8, 2 * HALF), 1)
    for f in range(FAR):
        wanted = []
        for d in range(NEAR):
            tail = x_ref[f, d // 4, ROWS - 8 :].astype(jnp.float32)
            tail = jnp.where(lane < HALF, pltpu.roll(tail, HALF, 1), tail)
            row = TAIL - ROWS + 8 + d % 4
            wanted.append(jnp.broadcast_to(tail[row : row + 1], (16, 2 * HALF)).astype(jnp.bfloat16))
        for k in range(0, ROWS, 16):
            n = min(16, ROWS - k)
            parts = [x_ref[f, t, k : k + n] for t in range(STATIONS)]
            for d in range(NEAR):
                best = parts[0]
                for t in range(1, STATIONS):
                    best = jnp.where(wanted[d][:n] == t, parts[t], best)
                out_ref[d, f, k : k + n] = best


def choose_call(x):
    vmem = pl.BlockSpec(memory_space=pltpu.VMEM)
    return pl.pallas_call(
        choose_kernel,
        out_shape=jax.ShapeDtypeStruct((NEAR, FAR, ROWS, 2 * HALF), jnp.bfloat16),
        in_specs=[vmem],
        out_specs=vmem,
        compiler_params=pltpu.CompilerParams(vmem_limit_bytes=48 * 2**20),
        name="choose",
    )(x)


def place(owner):
    return (owner & (NEAR - 1)) * FAR + (owner >> 4)


def lag_kernel(row_ref, w_ref, back_ref, twist_ref, lag_ref, out_ref, stage, gather, product):
    lane = lax.broadcasted_iota(jnp.int32, (ROWS, 2 * HALF), 1) % HALF
    s = w_ref[place(row_ref[0])].astype(jnp.float32)
    s1 = jnp.where(lane < KB, s, pltpu.roll(s, KB, 1)).astype(jnp.bfloat16)
    s2 = jnp.where(lane < KB, pltpu.roll(s, 2 * HALF - KB, 1), s).astype(jnp.bfloat16)
    scale = 1.0 / math.sqrt(KB * N2)

    for i in range(PAIRS):
        r = w_ref[place(row_ref[i + 1])]
        product[i, :ROWS] = jnp.concatenate([r * s1, r * s2], 1)
    both = product[...].reshape(PAIRS * PITCH, 4 * HALF)
    turned = [[] for _ in range(PAIRS)]
    for h in range(2):
        z = jnp.dot(
            both,
            back_ref[:, 2 * h * WIDE : 2 * (h + 1) * WIDE],
            preferred_element_type=jnp.float32,
        ).astype(jnp.bfloat16)
        cosine, sine = twist_ref[h, 0], twist_ref[h, 1]
        for i in range(PAIRS):
            mine = z[i * PITCH : i * PITCH + ROWS]
            re, im = mine[:, :WIDE], mine[:, WIDE:]
            a = re * cosine - im * sine
            b = re * sine + im * cosine
            turned[i].append(jnp.concatenate([a, b], 1))
    for i in range(PAIRS):
        total = jnp.dot(
            lag_ref[...],
            jnp.concatenate(turned[i], 0),
            preferred_element_type=jnp.float32,
        )
        re = (total[: 2 * H, :WIDE] - total[2 * H :, WIDE:]) * scale
        im = (total[2 * H :, :WIDE] + total[: 2 * H, WIDE:]) * scale
        at = pl.ds(i * 2 * H, 2 * H)
        for lanes in range(2):
            stage[lanes, at] = re[:, lanes * 128 : (lanes + 1) * 128]
            stage[2 + lanes, at] = im[:, lanes * 128 : (lanes + 1) * 128]

    gather[...] = jnp.zeros_like(gather)
    for j in range(H):
        for n in range(2):
            for lanes in range(4):
                rows = stage.at[lanes][pl.ds(2 * j + n, PAIRS, stride=2 * H)]
                gather[n * PAIRS : (n + 1) * PAIRS, lanes * 128 : (lanes + 1) * 128] = rows
        out_ref[j] = gather[...].astype(jnp.bfloat16)


def lag_call(rows, w):
    back, twist, lag = backward_tables()
    vmem = pl.BlockSpec(memory_space=pltpu.VMEM)
    return pl.pallas_call(
        lag_kernel,
        out_shape=jax.ShapeDtypeStruct((H, LAGROWS, 2 * WIDE), jnp.bfloat16),
        in_specs=[pl.BlockSpec(memory_space=pltpu.SMEM), vmem, vmem, vmem, vmem],
        out_specs=vmem,
        scratch_shapes=[
            pltpu.VMEM((4, PAIRS * 2 * H, 128), jnp.float32),
            pltpu.VMEM((LAGROWS, 2 * WIDE), jnp.float32),
            pltpu.VMEM((PAIRS, PITCH, 4 * HALF), jnp.bfloat16),
        ],
        compiler_params=pltpu.CompilerParams(vmem_limit_bytes=48 * 2**20),
        name="lags",
    )(rows, w, jnp.asarray(back), jnp.asarray(twist), jnp.asarray(lag))


def stack_kernel(x_ref, out_ref):
    segments = x_ref.shape[0]
    linear = jnp.zeros((LAGROWS, WIDE), jnp.float32)
    phase_re = jnp.zeros((LAGROWS, WIDE), jnp.float32)
    phase_im = jnp.zeros((LAGROWS, WIDE), jnp.float32)
    for s in range(segments):
        re = x_ref[s, :, :WIDE].astype(jnp.float32)
        im = x_ref[s, :, WIDE:].astype(jnp.float32)
        inverse = 1.0 / jnp.maximum(jnp.sqrt(re * re + im * im), 0.25)
        linear = linear + re
        phase_re = phase_re + re * inverse
        phase_im = phase_im + im * inverse
    coherence = jnp.sqrt(phase_re * phase_re + phase_im * phase_im)
    pws = linear * coherence * (1.0 / segments)
    out_ref[:, :N1] = pws[:PAIRS, :N1]
    out_ref[:, N1:] = pws[PAIRS : 2 * PAIRS, :N1]


def stack_call(x):
    vmem = pl.BlockSpec(memory_space=pltpu.VMEM)
    return pl.pallas_call(
        stack_kernel,
        out_shape=jax.ShapeDtypeStruct((PAIRS, 2 * N1), jnp.float32),
        in_specs=[vmem],
        out_specs=vmem,
        compiler_params=pltpu.CompilerParams(vmem_limit_bytes=48 * 2**20),
        name="stack",
    )(x)


def local(traces, block_sources, send_lists):
    pick = send_lists.reshape(-1)
    rows = block_sources.reshape(-1)
    whitened = spectrum_call(pick, traces)
    whitened = lax.all_to_all(whitened, "far", split_axis=0, concat_axis=0, tiled=True)
    chosen = choose_call(whitened)
    chosen = lax.all_to_all(chosen, ("near", "cell"), split_axis=0, concat_axis=0, tiled=True)
    lags = lag_call(rows, chosen.reshape(FAR * NEAR, ROWS, 2 * HALF))
    lags = lax.all_to_all(lags, "seg", split_axis=0, concat_axis=0, tiled=True)
    return stack_call(lags)


def solution(mesh):
    split = Mesh(mesh.devices.reshape(FAR, 2, NEAR // 2, -1), ("far", "near", "cell", "seg"))
    pairs = ("far", "near", "cell")
    return jax.shard_map(
        local,
        mesh=split,
        in_specs=(P("seg", pairs, None), P(pairs, None), P(pairs, None, None)),
        out_specs=P(pairs, "seg"),
        check_vma=False,
    )
```

```python
import math

import jax
import jax.numpy as jnp
import numpy as np
from jax import lax
from jax.experimental import pallas as pl
from jax.experimental.pallas import tpu as pltpu
from jax.sharding import Mesh
from jax.sharding import PartitionSpec as P

N1 = 240
N2 = 300
KB = 32
H = 8
ROWS = 152
HALF = 64
WIDE = 256
PAIRS = 25
PITCH = 160
LAGROWS = 8 * PAIRS
STATIONS = 4
FAR = 4
NEAR = 16
FOLD = 8
STEP = FOLD * N1
FULL = N2 // FOLD
STAGED = 40
TAIL = 148


def angles(left, right, period):
    product = (left[:, None] * right[None, :] % period).astype(np.float32)
    return product * np.float32(2.0 * math.pi / period)


def bf(table):
    return np.asarray(table, np.float32).astype(jnp.bfloat16)


def forward_tables():
    inner = np.arange(N2)
    outer = np.arange(N1)
    band = np.arange(1, KB + 1)
    a = angles(inner, inner, N2)
    dft = np.zeros((4 * ROWS, FOLD * STAGED), np.float32)
    column = inner % FOLD * STAGED + inner // FOLD
    dft[:N2, column] = np.cos(a)
    dft[2 * ROWS : 2 * ROWS + N2, column] = -np.sin(a)
    t = angles(inner, outer, N1 * N2)
    twist = np.zeros((2, 2 * ROWS, N1), np.float32)
    twist[0, :N2] = np.cos(t)
    twist[1, :N2] = np.sin(t)
    o = angles(outer, band, N1)
    c, s = np.cos(o), np.sin(o)
    last = np.stack([np.concatenate([c, -s, c, -s], 1), np.concatenate([s, c, s, c], 1)])
    return bf(dft), bf(twist), bf(last)


def backward_tables():
    inner = np.arange(N2)
    outer = np.arange(N1)
    band = np.arange(1, KB + 1)
    o = angles(band, outer, N1)
    c, s = np.cos(o), np.sin(o)
    back = np.zeros((4 * HALF, 4 * WIDE), np.float32)
    for h in range(2):
        row, col = h * HALF, 2 * h * WIDE
        re, im = slice(col, col + N1), slice(col + WIDE, col + WIDE + N1)
        for at, to_re, to_im in (
            (row, c, s),
            (row + KB, s, -c),
            (2 * HALF + row, -s, c),
            (2 * HALF + row + KB, c, s),
        ):
            back[at : at + KB, re] = to_re
            back[at : at + KB, im] = to_im
    t = angles(inner, outer, N1 * N2)
    twist = np.zeros((2, 2, ROWS, WIDE), np.float32)
    for h in range(2):
        n = min(ROWS, N2 - h * ROWS)
        twist[h, 0, :n, :N1] = np.cos(t[h * ROWS : h * ROWS + n])
        twist[h, 1, :n, :N1] = np.sin(t[h * ROWS : h * ROWS + n])
    l = angles(np.arange(-H, H) % N2, inner, N2)
    lag = np.zeros((2, 4 * H, ROWS), np.float32)
    for h in range(2):
        n = min(ROWS, N2 - h * ROWS)
        lag[h, : 2 * H, :n] = np.cos(l[:, h * ROWS : h * ROWS + n])
        lag[h, 2 * H :, :n] = np.sin(l[:, h * ROWS : h * ROWS + n])
    return bf(back), bf(twist), bf(np.concatenate([lag[0], lag[1]], 1))


def spectrum_kernel(
    pick_hbm, x_hbm, dft_hbm, twist_hbm, last_hbm, out_ref, pick_ref, x_ref, stage, dft_ref, twist_ref, last_ref, sems
):
    copies = [
        pltpu.make_async_copy(source, target, sems.at[i])
        for i, (source, target) in enumerate(
            (
                (x_hbm, x_ref),
                (dft_hbm, dft_ref),
                (twist_hbm, twist_ref),
                (last_hbm, last_ref),
                (pick_hbm, pick_ref),
            )
        )
    ]
    for copy in copies:
        copy.start()
    tiles = STEP // 128
    copies[0].wait()
    stage[:, STAGED * STATIONS - 16 :] = jnp.zeros((tiles, 16, 128), jnp.float32)
    for a in range(FULL):
        chunk = x_ref[0, :, a * STEP : (a + 1) * STEP].astype(jnp.float32)
        for c in range(tiles):
            stage[c, a * STATIONS : (a + 1) * STATIONS] = chunk[:, c * 128 : (c + 1) * 128]
    rest = x_ref[0, :, FULL * STEP :].astype(jnp.float32)
    rest = jnp.concatenate([rest, jnp.zeros((STATIONS, STEP - rest.shape[1]), jnp.float32)], 1)
    for c in range(tiles):
        stage[c, FULL * STATIONS : (FULL + 1) * STATIONS] = rest[:, c * 128 : (c + 1) * 128]
    for copy in copies[1:]:
        copy.wait()
    cosine = twist_ref[0].astype(jnp.float32)
    sine = twist_ref[1].astype(jnp.float32)
    lane = lax.broadcasted_iota(jnp.int32, (ROWS, 2 * HALF), 1)
    reals, imags = [], []
    for t in range(STATIONS):
        at = pl.ds(t, STAGED, stride=STATIONS)
        rows = jnp.concatenate([stage.at[c][at] for c in range(tiles)], 1)
        v = jnp.concatenate([rows[:, r * N1 : (r + 1) * N1] for r in range(FOLD)], 0)
        y = jnp.dot(dft_ref[...], v.astype(jnp.bfloat16), preferred_element_type=jnp.float32)
        re, im = y[: 2 * ROWS], y[2 * ROWS :]
        reals.append((re * cosine + im * sine).astype(jnp.bfloat16))
        imags.append((im * cosine - re * sine).astype(jnp.bfloat16))
    spectra = jnp.dot(jnp.concatenate(reals, 0), last_ref[0], preferred_element_type=jnp.float32)
    spectra = spectra + jnp.dot(jnp.concatenate(imags, 0), last_ref[1], preferred_element_type=jnp.float32)
    row = lax.broadcasted_iota(jnp.int32, (8, 2 * HALF), 0) + (ROWS - 8)
    upper = lax.broadcasted_iota(jnp.int32, (8, 2 * HALF), 1) >= HALF
    for t in range(STATIONS):
        x = spectra[2 * ROWS * t : 2 * ROWS * (t + 1)]
        power = x * x
        size = jnp.sqrt(power + pltpu.roll(power, KB, 1))
        level = jnp.sum(size, axis=0, keepdims=True) * (1.0 / N2) + 1e-6
        w = x * (1.0 / level)
        packed = jnp.where(lane < HALF, w[:ROWS], w[ROWS:])
        for f in range(FAR):
            tail = packed[ROWS - 8 :]
            for i in range(NEAR // STATIONS):
                wanted = pick_ref[f * NEAR + t * (NEAR // STATIONS) + i].astype(jnp.float32)
                tail = jnp.where((row == TAIL + i) & upper, wanted, tail)
            out_ref[f, t] = jnp.concatenate([packed[: ROWS - 8], tail], 0).astype(jnp.bfloat16)


def spectrum_call(pick, x):
    dft, twist, last = forward_tables()
    vmem = pl.BlockSpec(memory_space=pltpu.VMEM)
    hbm = pl.BlockSpec(memory_space=pl.ANY)
    return pl.pallas_call(
        spectrum_kernel,
        out_shape=jax.ShapeDtypeStruct((FAR, STATIONS, ROWS, 2 * HALF), jnp.bfloat16),
        in_specs=[hbm, hbm, hbm, hbm, hbm],
        out_specs=vmem,
        scratch_shapes=[
            pltpu.SMEM(pick.shape, jnp.int32),
            pltpu.VMEM(x.shape, jnp.bfloat16),
            pltpu.VMEM((STEP // 128, STAGED * STATIONS, 128), jnp.float32),
            pltpu.VMEM(dft.shape, jnp.bfloat16),
            pltpu.VMEM(twist.shape, jnp.bfloat16),
            pltpu.VMEM(last.shape, jnp.bfloat16),
            pltpu.SemaphoreType.DMA((5,)),
        ],
        compiler_params=pltpu.CompilerParams(vmem_limit_bytes=60 * 2**20),
        name="spectrum",
    )(pick, x, jnp.asarray(dft), jnp.asarray(twist), jnp.asarray(last))


def choose_kernel(x_ref, out_ref):
    lane = lax.broadcasted_iota(jnp.int32, (8, 2 * HALF), 1)
    for f in range(FAR):
        wanted = []
        for d in range(NEAR):
            tail = x_ref[f, d // 4, ROWS - 8 :].astype(jnp.float32)
            tail = jnp.where(lane < HALF, pltpu.roll(tail, HALF, 1), tail)
            row = TAIL - ROWS + 8 + d % 4
            wanted.append(jnp.broadcast_to(tail[row : row + 1], (16, 2 * HALF)).astype(jnp.bfloat16))
        for k in range(0, ROWS, 16):
            n = min(16, ROWS - k)
            parts = [x_ref[f, t, k : k + n] for t in range(STATIONS)]
            for d in range(NEAR):
                best = parts[0]
                for t in range(1, STATIONS):
                    best = jnp.where(wanted[d][:n] == t, parts[t], best)
                out_ref[d, f, k : k + n] = best


def choose_call(x):
    vmem = pl.BlockSpec(memory_space=pltpu.VMEM)
    return pl.pallas_call(
        choose_kernel,
        out_shape=jax.ShapeDtypeStruct((NEAR, FAR, ROWS, 2 * HALF), jnp.bfloat16),
        in_specs=[vmem],
        out_specs=vmem,
        compiler_params=pltpu.CompilerParams(vmem_limit_bytes=48 * 2**20),
        name="choose",
    )(x)


def place(owner):
    return (owner & (NEAR - 1)) * FAR + (owner >> 4)


def lag_kernel(row_ref, w_ref, back_ref, twist_ref, lag_ref, out_ref, stage, gather, product):
    lane = lax.broadcasted_iota(jnp.int32, (ROWS, 2 * HALF), 1) % HALF
    s = w_ref[place(row_ref[0])].astype(jnp.float32)
    s1 = jnp.where(lane < KB, s, pltpu.roll(s, KB, 1)).astype(jnp.bfloat16)
    s2 = jnp.where(lane < KB, pltpu.roll(s, 2 * HALF - KB, 1), s).astype(jnp.bfloat16)
    scale = 1.0 / math.sqrt(KB * N2)

    for i in range(PAIRS):
        r = w_ref[place(row_ref[i + 1])]
        product[i, :ROWS] = jnp.concatenate([r * s1, r * s2], 1)
    both = product[...].reshape(PAIRS * PITCH, 4 * HALF)
    turned = [[] for _ in range(PAIRS)]
    for h in range(2):
        z = jnp.dot(
            both,
            back_ref[:, 2 * h * WIDE : 2 * (h + 1) * WIDE],
            preferred_element_type=jnp.float32,
        ).astype(jnp.bfloat16)
        cosine, sine = twist_ref[h, 0], twist_ref[h, 1]
        for i in range(PAIRS):
            mine = z[i * PITCH : i * PITCH + ROWS]
            re, im = mine[:, :WIDE], mine[:, WIDE:]
            a = re * cosine - im * sine
            b = re * sine + im * cosine
            turned[i].append(jnp.concatenate([a, b], 1))
    for i in range(PAIRS):
        total = jnp.dot(
            lag_ref[...],
            jnp.concatenate(turned[i], 0),
            preferred_element_type=jnp.float32,
        )
        re = (total[: 2 * H, :WIDE] - total[2 * H :, WIDE:]) * scale
        im = (total[2 * H :, :WIDE] + total[: 2 * H, WIDE:]) * scale
        at = pl.ds(i * 2 * H, 2 * H)
        for lanes in range(2):
            stage[lanes, at] = re[:, lanes * 128 : (lanes + 1) * 128]
            stage[2 + lanes, at] = im[:, lanes * 128 : (lanes + 1) * 128]

    for j in range(H):
        for lanes in range(4):
            for n in range(2):
                rows = stage.at[lanes][pl.ds(2 * j + n, PAIRS, stride=2 * H)]
                gather[pl.ds((2 * lanes + n) * PAIRS, PAIRS)] = rows
        out_ref[j] = gather[...].astype(jnp.bfloat16)


def lag_call(rows, w):
    back, twist, lag = backward_tables()
    vmem = pl.BlockSpec(memory_space=pltpu.VMEM)
    return pl.pallas_call(
        lag_kernel,
        out_shape=jax.ShapeDtypeStruct((H, LAGROWS, 128), jnp.bfloat16),
        in_specs=[pl.BlockSpec(memory_space=pltpu.SMEM), vmem, vmem, vmem, vmem],
        out_specs=vmem,
        scratch_shapes=[
            pltpu.VMEM((4, PAIRS * 2 * H, 128), jnp.float32),
            pltpu.VMEM((LAGROWS, 128), jnp.float32),
            pltpu.VMEM((PAIRS, PITCH, 4 * HALF), jnp.bfloat16),
        ],
        compiler_params=pltpu.CompilerParams(vmem_limit_bytes=48 * 2**20),
        name="lags",
    )(rows, w, jnp.asarray(back), jnp.asarray(twist), jnp.asarray(lag))


def stack_kernel(x_ref, out_ref):
    segments = x_ref.shape[0]
    half = LAGROWS // 2
    linear = phase_re = phase_im = None
    for s in range(segments):
        x = x_ref[s].astype(jnp.float32)
        re, im = x[:half], x[half:]
        inverse = 1.0 / jnp.maximum(jnp.sqrt(re * re + im * im), 0.25)
        if s == 0:
            linear, phase_re, phase_im = re, re * inverse, im * inverse
        else:
            linear = linear + re
            phase_re = phase_re + re * inverse
            phase_im = phase_im + im * inverse
    coherence = jnp.sqrt(phase_re * phase_re + phase_im * phase_im)
    pws = linear * coherence * (1.0 / segments)
    for n in range(2):
        low = pws[n * PAIRS : (n + 1) * PAIRS]
        high = pws[(2 + n) * PAIRS : (3 + n) * PAIRS]
        out_ref[:, n * N1 : (n + 1) * N1] = jnp.concatenate([low, high], 1)[:, :N1]


def stack_call(x):
    vmem = pl.BlockSpec(memory_space=pltpu.VMEM)
    return pl.pallas_call(
        stack_kernel,
        out_shape=jax.ShapeDtypeStruct((PAIRS, 2 * N1), jnp.float32),
        in_specs=[vmem],
        out_specs=vmem,
        compiler_params=pltpu.CompilerParams(vmem_limit_bytes=48 * 2**20),
        name="stack",
    )(x)


def local(traces, block_sources, send_lists):
    pick = send_lists.reshape(-1)
    rows = block_sources.reshape(-1)
    whitened = spectrum_call(pick, traces)
    whitened = lax.all_to_all(whitened, "far", split_axis=0, concat_axis=0, tiled=True)
    chosen = choose_call(whitened)
    chosen = lax.all_to_all(chosen, ("near", "cell"), split_axis=0, concat_axis=0, tiled=True)
    lags = lag_call(rows, chosen.reshape(FAR * NEAR, ROWS, 2 * HALF))
    lags = lax.all_to_all(lags, "seg", split_axis=0, concat_axis=0, tiled=True)
    return stack_call(lags)


def solution(mesh):
    split = Mesh(mesh.devices.reshape(FAR, 2, NEAR // 2, -1), ("far", "near", "cell", "seg"))
    pairs = ("far", "near", "cell")
    return jax.shard_map(
        local,
        mesh=split,
        in_specs=(P("seg", pairs, None), P(pairs, None), P(pairs, None, None)),
        out_specs=P(pairs, "seg"),
        check_vma=False,
    )
```

```python
import math

import jax
import jax.numpy as jnp
import numpy as np
from jax import lax
from jax.experimental import pallas as pl
from jax.experimental.pallas import tpu as pltpu
from jax.sharding import Mesh
from jax.sharding import PartitionSpec as P

N1 = 240
N2 = 300
KB = 32
H = 8
ROWS = 152
HALF = 64
WIDE = 256
PAIRS = 25
PITCH = 160
LAGROWS = 8 * PAIRS
STATIONS = 4
FAR = 4
NEAR = 16
FOLD = 8
STEP = FOLD * N1
FULL = N2 // FOLD
STAGED = 40
TAIL = 148


def angles(left, right, period):
    product = (left[:, None] * right[None, :] % period).astype(np.float32)
    return product * np.float32(2.0 * math.pi / period)


def bf(table):
    return np.asarray(table, np.float32).astype(jnp.bfloat16)


def forward_tables():
    inner = np.arange(N2)
    outer = np.arange(N1)
    band = np.arange(1, KB + 1)
    a = angles(inner, inner, N2)
    dft = np.zeros((4 * ROWS, FOLD * STAGED), np.float32)
    column = inner % FOLD * STAGED + inner // FOLD
    dft[:N2, column] = np.cos(a)
    dft[2 * ROWS : 2 * ROWS + N2, column] = -np.sin(a)
    t = angles(inner, outer, N1 * N2)
    twist = np.zeros((2, 2 * ROWS, N1), np.float32)
    twist[0, :N2] = np.cos(t)
    twist[1, :N2] = np.sin(t)
    o = angles(outer, band, N1)
    c, s = np.cos(o), np.sin(o)
    last = np.stack([np.concatenate([c, -s, c, -s], 1), np.concatenate([s, c, s, c], 1)])
    return bf(dft), bf(twist), bf(last)


def backward_tables():
    inner = np.arange(N2)
    outer = np.arange(N1)
    band = np.arange(1, KB + 1)
    o = angles(band, outer, N1)
    c, s = np.cos(o), np.sin(o)
    back = np.zeros((4 * HALF, 4 * WIDE), np.float32)
    for h in range(2):
        row, col = h * HALF, 2 * h * WIDE
        re, im = slice(col, col + N1), slice(col + WIDE, col + WIDE + N1)
        for at, to_re, to_im in (
            (row, c, s),
            (row + KB, s, -c),
            (2 * HALF + row, -s, c),
            (2 * HALF + row + KB, c, s),
        ):
            back[at : at + KB, re] = to_re
            back[at : at + KB, im] = to_im
    t = angles(inner, outer, N1 * N2)
    twist = np.zeros((2, 2, ROWS, WIDE), np.float32)
    for h in range(2):
        n = min(ROWS, N2 - h * ROWS)
        twist[h, 0, :n, :N1] = np.cos(t[h * ROWS : h * ROWS + n])
        twist[h, 1, :n, :N1] = np.sin(t[h * ROWS : h * ROWS + n])
    l = angles(np.arange(-H, H) % N2, inner, N2)
    lag = np.zeros((2, 4 * H, ROWS), np.float32)
    for h in range(2):
        n = min(ROWS, N2 - h * ROWS)
        lag[h, : 2 * H, :n] = np.cos(l[:, h * ROWS : h * ROWS + n])
        lag[h, 2 * H :, :n] = np.sin(l[:, h * ROWS : h * ROWS + n])
    return bf(back), bf(twist), bf(np.concatenate([lag[0], lag[1]], 1))


def spectrum_kernel(
    pick_hbm, x_hbm, dft_hbm, twist_hbm, last_hbm, out_ref, pick_ref, x_ref, stage, dft_ref, twist_ref, last_ref, sems
):
    copies = [
        pltpu.make_async_copy(source, target, sems.at[i])
        for i, (source, target) in enumerate(
            (
                (x_hbm, x_ref),
                (dft_hbm, dft_ref),
                (twist_hbm, twist_ref),
                (last_hbm, last_ref),
                (pick_hbm, pick_ref),
            )
        )
    ]
    for copy in copies:
        copy.start()
    tiles = STEP // 128
    copies[0].wait()
    stage[:, STAGED * STATIONS - 16 :] = jnp.zeros((tiles, 16, 128), jnp.float32)
    for a in range(FULL):
        chunk = x_ref[0, :, a * STEP : (a + 1) * STEP].astype(jnp.float32)
        for c in range(tiles):
            stage[c, a * STATIONS : (a + 1) * STATIONS] = chunk[:, c * 128 : (c + 1) * 128]
    rest = x_ref[0, :, FULL * STEP :].astype(jnp.float32)
    rest = jnp.concatenate([rest, jnp.zeros((STATIONS, STEP - rest.shape[1]), jnp.float32)], 1)
    for c in range(tiles):
        stage[c, FULL * STATIONS : (FULL + 1) * STATIONS] = rest[:, c * 128 : (c + 1) * 128]
    for copy in copies[1:]:
        copy.wait()
    cosine = twist_ref[0].astype(jnp.float32)
    sine = twist_ref[1].astype(jnp.float32)
    lane = lax.broadcasted_iota(jnp.int32, (ROWS, 2 * HALF), 1)
    reals, imags = [], []
    for t in range(STATIONS):
        at = pl.ds(t, STAGED, stride=STATIONS)
        rows = jnp.concatenate([stage.at[c][at] for c in range(tiles)], 1)
        v = jnp.concatenate([rows[:, r * N1 : (r + 1) * N1] for r in range(FOLD)], 0)
        y = jnp.dot(dft_ref[...], v.astype(jnp.bfloat16), preferred_element_type=jnp.float32)
        re, im = y[: 2 * ROWS], y[2 * ROWS :]
        reals.append((re * cosine + im * sine).astype(jnp.bfloat16))
        imags.append((im * cosine - re * sine).astype(jnp.bfloat16))
    spectra = jnp.dot(jnp.concatenate(reals, 0), last_ref[0], preferred_element_type=jnp.float32)
    spectra = spectra + jnp.dot(jnp.concatenate(imags, 0), last_ref[1], preferred_element_type=jnp.float32)
    row = lax.broadcasted_iota(jnp.int32, (8, 2 * HALF), 0) + (ROWS - 8)
    upper = lax.broadcasted_iota(jnp.int32, (8, 2 * HALF), 1) >= HALF
    for t in range(STATIONS):
        x = spectra[2 * ROWS * t : 2 * ROWS * (t + 1)]
        power = x * x
        size = jnp.sqrt(power + pltpu.roll(power, KB, 1))
        level = jnp.sum(size, axis=0, keepdims=True) * (1.0 / N2) + 1e-6
        w = x * (1.0 / level)
        packed = jnp.where(lane < HALF, w[:ROWS], w[ROWS:])
        for f in range(FAR):
            tail = packed[ROWS - 8 :]
            for i in range(NEAR // STATIONS):
                wanted = pick_ref[f * NEAR + t * (NEAR // STATIONS) + i].astype(jnp.float32)
                tail = jnp.where((row == TAIL + i) & upper, wanted, tail)
            out_ref[f, t] = jnp.concatenate([packed[: ROWS - 8], tail], 0).astype(jnp.bfloat16)


def spectrum_call(pick, x):
    dft, twist, last = forward_tables()
    vmem = pl.BlockSpec(memory_space=pltpu.VMEM)
    hbm = pl.BlockSpec(memory_space=pl.ANY)
    return pl.pallas_call(
        spectrum_kernel,
        out_shape=pltpu.VMEM((FAR, STATIONS, ROWS, 2 * HALF), jnp.bfloat16),
        in_specs=[hbm, hbm, hbm, hbm, hbm],
        out_specs=vmem,
        scratch_shapes=[
            pltpu.SMEM(pick.shape, jnp.int32),
            pltpu.VMEM(x.shape, jnp.bfloat16),
            pltpu.VMEM((STEP // 128, STAGED * STATIONS, 128), jnp.float32),
            pltpu.VMEM(dft.shape, jnp.bfloat16),
            pltpu.VMEM(twist.shape, jnp.bfloat16),
            pltpu.VMEM(last.shape, jnp.bfloat16),
            pltpu.SemaphoreType.DMA((5,)),
        ],
        compiler_params=pltpu.CompilerParams(vmem_limit_bytes=56 * 2**20),
        name="spectrum",
    )(pick, x, jnp.asarray(dft), jnp.asarray(twist), jnp.asarray(last))


def choose_kernel(x_ref, out_ref):
    lane = lax.broadcasted_iota(jnp.int32, (8, 2 * HALF), 1)
    for f in range(FAR):
        wanted = []
        for d in range(NEAR):
            tail = x_ref[f, d // 4, ROWS - 8 :].astype(jnp.float32)
            tail = jnp.where(lane < HALF, pltpu.roll(tail, HALF, 1), tail)
            row = TAIL - ROWS + 8 + d % 4
            wanted.append(jnp.broadcast_to(tail[row : row + 1], (16, 2 * HALF)).astype(jnp.bfloat16))
        for k in range(0, ROWS, 16):
            n = min(16, ROWS - k)
            parts = [x_ref[f, t, k : k + n] for t in range(STATIONS)]
            for d in range(NEAR):
                best = parts[0]
                for t in range(1, STATIONS):
                    best = jnp.where(wanted[d][:n] == t, parts[t], best)
                out_ref[d, f, k : k + n] = best


def choose_call(x):
    vmem = pl.BlockSpec(memory_space=pltpu.VMEM)
    return pl.pallas_call(
        choose_kernel,
        out_shape=jax.ShapeDtypeStruct((NEAR, FAR, ROWS, 2 * HALF), jnp.bfloat16),
        in_specs=[vmem],
        out_specs=vmem,
        compiler_params=pltpu.CompilerParams(vmem_limit_bytes=48 * 2**20),
        name="choose",
    )(x)


def place(owner):
    return (owner & (NEAR - 1)) * FAR + (owner >> 4)


def lag_kernel(row_ref, w_ref, back_ref, twist_ref, lag_ref, out_ref, stage, gather, product):
    lane = lax.broadcasted_iota(jnp.int32, (ROWS, 2 * HALF), 1) % HALF
    s = w_ref[place(row_ref[0])].astype(jnp.float32)
    s1 = jnp.where(lane < KB, s, pltpu.roll(s, KB, 1)).astype(jnp.bfloat16)
    s2 = jnp.where(lane < KB, pltpu.roll(s, 2 * HALF - KB, 1), s).astype(jnp.bfloat16)
    scale = 1.0 / math.sqrt(KB * N2)

    for i in range(PAIRS):
        r = w_ref[place(row_ref[i + 1])]
        product[i, :ROWS] = jnp.concatenate([r * s1, r * s2], 1)
    both = product[...].reshape(PAIRS * PITCH, 4 * HALF)
    turned = [[] for _ in range(PAIRS)]
    for h in range(2):
        z = jnp.dot(
            both,
            back_ref[:, 2 * h * WIDE : 2 * (h + 1) * WIDE],
            preferred_element_type=jnp.float32,
        ).astype(jnp.bfloat16)
        cosine, sine = twist_ref[h, 0], twist_ref[h, 1]
        for i in range(PAIRS):
            mine = z[i * PITCH : i * PITCH + ROWS]
            re, im = mine[:, :WIDE], mine[:, WIDE:]
            a = re * cosine - im * sine
            b = re * sine + im * cosine
            turned[i].append(jnp.concatenate([a, b], 1))
    for i in range(PAIRS):
        total = jnp.dot(
            lag_ref[...],
            jnp.concatenate(turned[i], 0),
            preferred_element_type=jnp.float32,
        )
        re = (total[: 2 * H, :WIDE] - total[2 * H :, WIDE:]) * scale
        im = (total[2 * H :, :WIDE] + total[: 2 * H, WIDE:]) * scale
        at = pl.ds(i * 2 * H, 2 * H)
        for lanes in range(2):
            stage[lanes, at] = re[:, lanes * 128 : (lanes + 1) * 128]
            stage[2 + lanes, at] = im[:, lanes * 128 : (lanes + 1) * 128]

    for j in range(H):
        for lanes in range(4):
            for n in range(2):
                rows = stage.at[lanes][pl.ds(2 * j + n, PAIRS, stride=2 * H)]
                gather[pl.ds((2 * lanes + n) * PAIRS, PAIRS)] = rows
        out_ref[j] = gather[...].astype(jnp.bfloat16)


def lag_call(rows, w):
    back, twist, lag = backward_tables()
    vmem = pl.BlockSpec(memory_space=pltpu.VMEM)
    return pl.pallas_call(
        lag_kernel,
        out_shape=jax.ShapeDtypeStruct((H, LAGROWS, 128), jnp.bfloat16),
        in_specs=[pl.BlockSpec(memory_space=pltpu.SMEM), vmem, vmem, vmem, vmem],
        out_specs=vmem,
        scratch_shapes=[
            pltpu.VMEM((4, PAIRS * 2 * H, 128), jnp.float32),
            pltpu.VMEM((LAGROWS, 128), jnp.float32),
            pltpu.VMEM((PAIRS, PITCH, 4 * HALF), jnp.bfloat16),
        ],
        compiler_params=pltpu.CompilerParams(vmem_limit_bytes=48 * 2**20),
        name="lags",
    )(rows, w, jnp.asarray(back), jnp.asarray(twist), jnp.asarray(lag))


def stack_kernel(x_ref, out_ref):
    segments = x_ref.shape[0]
    half = LAGROWS // 2
    linear = phase_re = phase_im = None
    for s in range(segments):
        x = x_ref[s].astype(jnp.float32)
        re, im = x[:half], x[half:]
        inverse = 1.0 / jnp.maximum(jnp.sqrt(re * re + im * im), 0.25)
        if s == 0:
            linear, phase_re, phase_im = re, re * inverse, im * inverse
        else:
            linear = linear + re
            phase_re = phase_re + re * inverse
            phase_im = phase_im + im * inverse
    coherence = jnp.sqrt(phase_re * phase_re + phase_im * phase_im)
    pws = linear * coherence * (1.0 / segments)
    for n in range(2):
        low = pws[n * PAIRS : (n + 1) * PAIRS]
        high = pws[(2 + n) * PAIRS : (3 + n) * PAIRS]
        out_ref[:, n * N1 : (n + 1) * N1] = jnp.concatenate([low, high], 1)[:, :N1]


def stack_call(x):
    vmem = pl.BlockSpec(memory_space=pltpu.VMEM)
    return pl.pallas_call(
        stack_kernel,
        out_shape=jax.ShapeDtypeStruct((PAIRS, 2 * N1), jnp.float32),
        in_specs=[vmem],
        out_specs=vmem,
        compiler_params=pltpu.CompilerParams(vmem_limit_bytes=48 * 2**20),
        name="stack",
    )(x)


def local(traces, block_sources, send_lists):
    pick = send_lists.reshape(-1)
    rows = block_sources.reshape(-1)
    whitened = spectrum_call(pick, traces)
    whitened = lax.all_to_all(whitened, "far", split_axis=0, concat_axis=0, tiled=True)
    chosen = choose_call(whitened)
    chosen = lax.all_to_all(chosen, ("near", "cell"), split_axis=0, concat_axis=0, tiled=True)
    lags = lag_call(rows, chosen.reshape(FAR * NEAR, ROWS, 2 * HALF))
    lags = lax.all_to_all(lags, "seg", split_axis=0, concat_axis=0, tiled=True)
    return stack_call(lags)


def solution(mesh):
    split = Mesh(mesh.devices.reshape(FAR, 2, NEAR // 2, -1), ("far", "near", "cell", "seg"))
    pairs = ("far", "near", "cell")
    return jax.shard_map(
        local,
        mesh=split,
        in_specs=(P("seg", pairs, None), P(pairs, None), P(pairs, None, None)),
        out_specs=P(pairs, "seg"),
        check_vma=False,
    )
```

```python
import math

import jax
import jax.numpy as jnp
import numpy as np
from jax import lax
from jax.experimental import pallas as pl
from jax.experimental.pallas import tpu as pltpu
from jax.sharding import Mesh
from jax.sharding import PartitionSpec as P

N1 = 240
N2 = 300
KB = 32
H = 8
ROWS = 152
HALF = 64
WIDE = 256
PAIRS = 25
PITCH = 160
LAGROWS = 8 * PAIRS
STATIONS = 4
FAR = 4
NEAR = 16
FOLD = 8
STEP = FOLD * N1
FULL = N2 // FOLD
STAGED = 40
MID = N2 // 2


def angles(left, right, period):
    product = (left[:, None] * right[None, :] % period).astype(np.float32)
    return product * np.float32(2.0 * math.pi / period)


def bf(table):
    return np.asarray(table, np.float32).astype(jnp.bfloat16)


def bins(h):
    at = np.arange(h, MID + 1 - h)
    return at, (N2 - at if h else at)


def forward_tables():
    inner = np.arange(N2)
    outer = np.arange(N1)
    band = np.arange(1, KB + 1)
    a = angles(inner, inner, N2)
    dft = np.zeros((2 * ROWS, FOLD * STAGED), np.float32)
    column = inner % FOLD * STAGED + inner // FOLD
    dft[: MID + 1, column] = np.cos(a[: MID + 1])
    dft[ROWS : ROWS + MID + 1, column] = -np.sin(a[: MID + 1])
    t = angles(inner, outer, N1 * N2)
    twist = np.zeros((2, 2, ROWS, N1), np.float32)
    for h in range(2):
        at, k2 = bins(h)
        twist[h, 0, at] = np.cos(t[k2])
        twist[h, 1, at] = np.sin(t[k2])
    o = angles(outer, band, N1)
    c, s = np.cos(o), np.sin(o)
    last = np.stack([np.concatenate([c, -s, c, -s], 1), np.concatenate([s, c, s, c], 1)])
    return bf(dft), bf(twist), bf(last)


def backward_tables():
    inner = np.arange(N2)
    outer = np.arange(N1)
    band = np.arange(1, KB + 1)
    o = angles(band, outer, N1)
    c, s = np.cos(o), np.sin(o)
    back = np.zeros((4 * HALF, 4 * WIDE), np.float32)
    for h in range(2):
        row, col = h * HALF, 2 * h * WIDE
        re, im = slice(col, col + N1), slice(col + WIDE, col + WIDE + N1)
        for at, to_re, to_im in (
            (row, c, s),
            (row + KB, s, -c),
            (2 * HALF + row, -s, c),
            (2 * HALF + row + KB, c, s),
        ):
            back[at : at + KB, re] = to_re
            back[at : at + KB, im] = to_im
    t = angles(inner, outer, N1 * N2)
    twist = np.zeros((2, 2, ROWS, WIDE), np.float32)
    for h in range(2):
        at, k2 = bins(h)
        twist[h, 0, at, :N1] = np.cos(t[k2])
        twist[h, 1, at, :N1] = np.sin(t[k2])
    l = angles(np.arange(-H, H) % N2, inner, N2)
    lag = np.zeros((2, 4 * H, ROWS), np.float32)
    for h in range(2):
        at, k2 = bins(h)
        lag[h, : 2 * H, at] = np.cos(l[:, k2]).T
        lag[h, 2 * H :, at] = np.sin(l[:, k2]).T
    return bf(back), bf(twist), bf(np.concatenate([lag[0], lag[1]], 1))


def spectrum_kernel(
    pick_hbm, x_hbm, dft_hbm, twist_hbm, last_hbm, out_ref, pick_ref, x_ref, stage, dft_ref, twist_ref, last_ref, sems
):
    copies = [
        pltpu.make_async_copy(source, target, sems.at[i])
        for i, (source, target) in enumerate(
            (
                (x_hbm, x_ref),
                (dft_hbm, dft_ref),
                (twist_hbm, twist_ref),
                (last_hbm, last_ref),
                (pick_hbm, pick_ref),
            )
        )
    ]
    for copy in copies:
        copy.start()
    tiles = STEP // 128
    copies[0].wait()
    stage[:, STAGED * STATIONS - 16 :] = jnp.zeros((tiles, 16, 128), jnp.float32)
    for a in range(FULL):
        chunk = x_ref[0, :, a * STEP : (a + 1) * STEP].astype(jnp.float32)
        for c in range(tiles):
            stage[c, a * STATIONS : (a + 1) * STATIONS] = chunk[:, c * 128 : (c + 1) * 128]
    rest = x_ref[0, :, FULL * STEP :].astype(jnp.float32)
    rest = jnp.concatenate([rest, jnp.zeros((STATIONS, STEP - rest.shape[1]), jnp.float32)], 1)
    for c in range(tiles):
        stage[c, FULL * STATIONS : (FULL + 1) * STATIONS] = rest[:, c * 128 : (c + 1) * 128]
    for copy in copies[1:]:
        copy.wait()
    turns = [[twist_ref[h, i].astype(jnp.float32) for i in range(2)] for h in range(2)]
    lane = lax.broadcasted_iota(jnp.int32, (ROWS, 2 * HALF), 1)
    reals, imags = [], []
    for t in range(STATIONS):
        at = pl.ds(t, STAGED, stride=STATIONS)
        rows = jnp.concatenate([stage.at[c][at] for c in range(tiles)], 1)
        v = jnp.concatenate([rows[:, r * N1 : (r + 1) * N1] for r in range(FOLD)], 0)
        y = jnp.dot(dft_ref[...], v.astype(jnp.bfloat16), preferred_element_type=jnp.float32)
        re, im = y[:ROWS], y[ROWS:]
        for (cosine, sine), conjugate in zip(turns, (im, -im)):
            reals.append((re * cosine + conjugate * sine).astype(jnp.bfloat16))
            imags.append((conjugate * cosine - re * sine).astype(jnp.bfloat16))
    spectra = jnp.dot(jnp.concatenate(reals, 0), last_ref[0], preferred_element_type=jnp.float32)
    spectra = spectra + jnp.dot(jnp.concatenate(imags, 0), last_ref[1], preferred_element_type=jnp.float32)
    row = lax.broadcasted_iota(jnp.int32, (8, 2 * HALF), 0)
    upper = lax.broadcasted_iota(jnp.int32, (8, 2 * HALF), 1) >= HALF
    spare = [(row == 0) & upper, (row == 6) & upper, (row == 7) & upper, (row == 7) & ~upper]
    for t in range(STATIONS):
        x = spectra[2 * ROWS * t : 2 * ROWS * (t + 1)]
        power = x * x
        size = jnp.sqrt(power + pltpu.roll(power, KB, 1))
        level = jnp.sum(size, axis=0, keepdims=True) * (1.0 / N2) + 1e-6
        w = x * (1.0 / level)
        packed = jnp.where(lane < HALF, w[:ROWS], w[ROWS:])
        for f in range(FAR):
            ends = [packed[:8], packed[ROWS - 8 :]]
            for i in range(NEAR // STATIONS):
                wanted = pick_ref[f * NEAR + t * (NEAR // STATIONS) + i].astype(jnp.float32)
                ends[i > 0] = jnp.where(spare[i], wanted, ends[i > 0])
            whole = jnp.concatenate([ends[0], packed[8 : ROWS - 8], ends[1]], 0)
            out_ref[f, t] = whole.astype(jnp.bfloat16)


def spectrum_call(pick, x):
    dft, twist, last = forward_tables()
    vmem = pl.BlockSpec(memory_space=pltpu.VMEM)
    hbm = pl.BlockSpec(memory_space=pl.ANY)
    return pl.pallas_call(
        spectrum_kernel,
        out_shape=pltpu.VMEM((FAR, STATIONS, ROWS, 2 * HALF), jnp.bfloat16),
        in_specs=[hbm, hbm, hbm, hbm, hbm],
        out_specs=vmem,
        scratch_shapes=[
            pltpu.SMEM(pick.shape, jnp.int32),
            pltpu.VMEM(x.shape, jnp.bfloat16),
            pltpu.VMEM((STEP // 128, STAGED * STATIONS, 128), jnp.float32),
            pltpu.VMEM(dft.shape, jnp.bfloat16),
            pltpu.VMEM(twist.shape, jnp.bfloat16),
            pltpu.VMEM(last.shape, jnp.bfloat16),
            pltpu.SemaphoreType.DMA((5,)),
        ],
        compiler_params=pltpu.CompilerParams(vmem_limit_bytes=56 * 2**20),
        name="spectrum",
    )(pick, x, jnp.asarray(dft), jnp.asarray(twist), jnp.asarray(last))


def choose_kernel(x_ref, out_ref):
    lane = lax.broadcasted_iota(jnp.int32, (8, 2 * HALF), 1)
    for f in range(FAR):
        wanted = []
        for t in range(STATIONS):
            head = x_ref[f, t, :16].astype(jnp.float32)[:8]
            tail = x_ref[f, t, ROWS - 8 :].astype(jnp.float32)
            head = jnp.where(lane < HALF, pltpu.roll(head, HALF, 1), head)
            turned = pltpu.roll(tail, HALF, 1)
            upper = jnp.where(lane < HALF, turned, tail)
            lower = jnp.where(lane < HALF, tail, turned)
            for line in (head[:1], upper[6:7], upper[7:], lower[7:]):
                wanted.append(jnp.broadcast_to(line, (16, 2 * HALF)).astype(jnp.bfloat16))
        for k in range(0, ROWS, 16):
            n = min(16, ROWS - k)
            parts = [x_ref[f, t, k : k + n] for t in range(STATIONS)]
            for d in range(NEAR):
                best = parts[0]
                for t in range(1, STATIONS):
                    best = jnp.where(wanted[d][:n] == t, parts[t], best)
                out_ref[d, f, k : k + n] = best


def choose_call(x):
    vmem = pl.BlockSpec(memory_space=pltpu.VMEM)
    return pl.pallas_call(
        choose_kernel,
        out_shape=jax.ShapeDtypeStruct((NEAR, FAR, ROWS, 2 * HALF), jnp.bfloat16),
        in_specs=[vmem],
        out_specs=vmem,
        compiler_params=pltpu.CompilerParams(vmem_limit_bytes=48 * 2**20),
        name="choose",
    )(x)


def place(owner):
    return (owner & (NEAR - 1)) * FAR + (owner >> 4)


def lag_kernel(row_ref, w_ref, back_ref, twist_ref, lag_ref, out_ref, stage, gather, product):
    lane = lax.broadcasted_iota(jnp.int32, (ROWS, 2 * HALF), 1) % HALF
    s = w_ref[place(row_ref[0])].astype(jnp.float32)
    s1 = jnp.where(lane < KB, s, pltpu.roll(s, KB, 1)).astype(jnp.bfloat16)
    s2 = jnp.where(lane < KB, pltpu.roll(s, 2 * HALF - KB, 1), s).astype(jnp.bfloat16)
    scale = 1.0 / math.sqrt(KB * N2)

    for i in range(PAIRS):
        r = w_ref[place(row_ref[i + 1])]
        product[i, :ROWS] = jnp.concatenate([r * s1, r * s2], 1)
    both = product[...].reshape(PAIRS * PITCH, 4 * HALF)
    turned = [[] for _ in range(PAIRS)]
    for h in range(2):
        z = jnp.dot(
            both,
            back_ref[:, 2 * h * WIDE : 2 * (h + 1) * WIDE],
            preferred_element_type=jnp.float32,
        ).astype(jnp.bfloat16)
        cosine, sine = twist_ref[h, 0], twist_ref[h, 1]
        for i in range(PAIRS):
            mine = z[i * PITCH : i * PITCH + ROWS]
            re, im = mine[:, :WIDE], mine[:, WIDE:]
            a = re * cosine - im * sine
            b = re * sine + im * cosine
            turned[i].append(jnp.concatenate([a, b], 1))
    for i in range(PAIRS):
        total = jnp.dot(
            lag_ref[...],
            jnp.concatenate(turned[i], 0),
            preferred_element_type=jnp.float32,
        )
        re = (total[: 2 * H, :WIDE] - total[2 * H :, WIDE:]) * scale
        im = (total[2 * H :, :WIDE] + total[: 2 * H, WIDE:]) * scale
        at = pl.ds(i * 2 * H, 2 * H)
        for lanes in range(2):
            stage[lanes, at] = re[:, lanes * 128 : (lanes + 1) * 128]
            stage[2 + lanes, at] = im[:, lanes * 128 : (lanes + 1) * 128]

    for j in range(H):
        for lanes in range(4):
            for n in range(2):
                rows = stage.at[lanes][pl.ds(2 * j + n, PAIRS, stride=2 * H)]
                gather[pl.ds((2 * lanes + n) * PAIRS, PAIRS)] = rows
        out_ref[j] = gather[...].astype(jnp.bfloat16)


def lag_call(rows, w):
    back, twist, lag = backward_tables()
    vmem = pl.BlockSpec(memory_space=pltpu.VMEM)
    return pl.pallas_call(
        lag_kernel,
        out_shape=jax.ShapeDtypeStruct((H, LAGROWS, 128), jnp.bfloat16),
        in_specs=[pl.BlockSpec(memory_space=pltpu.SMEM), vmem, vmem, vmem, vmem],
        out_specs=vmem,
        scratch_shapes=[
            pltpu.VMEM((4, PAIRS * 2 * H, 128), jnp.float32),
            pltpu.VMEM((LAGROWS, 128), jnp.float32),
            pltpu.VMEM((PAIRS, PITCH, 4 * HALF), jnp.bfloat16),
        ],
        compiler_params=pltpu.CompilerParams(vmem_limit_bytes=48 * 2**20),
        name="lags",
    )(rows, w, jnp.asarray(back), jnp.asarray(twist), jnp.asarray(lag))


def stack_kernel(x_ref, out_ref):
    segments = x_ref.shape[0]
    half = LAGROWS // 2
    linear = phase_re = phase_im = None
    for s in range(segments):
        x = x_ref[s].astype(jnp.float32)
        re, im = x[:half], x[half:]
        inverse = jnp.minimum(lax.rsqrt(re * re + im * im), 4.0)
        if s == 0:
            linear, phase_re, phase_im = re, re * inverse, im * inverse
        else:
            linear = linear + re
            phase_re = phase_re + re * inverse
            phase_im = phase_im + im * inverse
    coherence = jnp.sqrt(phase_re * phase_re + phase_im * phase_im)
    pws = linear * coherence * (1.0 / segments)
    for n in range(2):
        low = pws[n * PAIRS : (n + 1) * PAIRS]
        high = pws[(2 + n) * PAIRS : (3 + n) * PAIRS]
        out_ref[:, n * N1 : (n + 1) * N1] = jnp.concatenate([low, high], 1)[:, :N1]


def stack_call(x):
    vmem = pl.BlockSpec(memory_space=pltpu.VMEM)
    return pl.pallas_call(
        stack_kernel,
        out_shape=jax.ShapeDtypeStruct((PAIRS, 2 * N1), jnp.float32),
        in_specs=[vmem],
        out_specs=vmem,
        compiler_params=pltpu.CompilerParams(vmem_limit_bytes=48 * 2**20),
        name="stack",
    )(x)


def local(traces, block_sources, send_lists):
    pick = send_lists.reshape(-1)
    rows = block_sources.reshape(-1)
    whitened = spectrum_call(pick, traces)
    whitened = lax.all_to_all(whitened, "far", split_axis=0, concat_axis=0, tiled=True)
    chosen = choose_call(whitened)
    chosen = lax.all_to_all(chosen, ("near", "cell"), split_axis=0, concat_axis=0, tiled=True)
    lags = lag_call(rows, chosen.reshape(FAR * NEAR, ROWS, 2 * HALF))
    lags = lax.all_to_all(lags, "seg", split_axis=0, concat_axis=0, tiled=True)
    return stack_call(lags)


def solution(mesh):
    split = Mesh(mesh.devices.reshape(FAR, 2, NEAR // 2, -1), ("far", "near", "cell", "seg"))
    pairs = ("far", "near", "cell")
    return jax.shard_map(
        local,
        mesh=split,
        in_specs=(P("seg", pairs, None), P(pairs, None), P(pairs, None, None)),
        out_specs=P(pairs, "seg"),
        check_vma=False,
    )
```

```python
import math

import jax
import jax.numpy as jnp
import numpy as np
from jax import lax
from jax.experimental import pallas as pl
from jax.experimental.pallas import tpu as pltpu
from jax.sharding import Mesh
from jax.sharding import PartitionSpec as P

N1 = 240
N2 = 300
KB = 32
H = 8
ROWS = 152
HALF = 64
WIDE = 256
PAIRS = 25
PITCH = 160
LAGROWS = 8 * PAIRS
STATIONS = 4
FAR = 4
NEAR = 16
FOLD = 8
STEP = FOLD * N1
FULL = N2 // FOLD
STAGED = 40
MID = N2 // 2


def angles(left, right, period):
    product = (left[:, None] * right[None, :] % period).astype(np.float32)
    return product * np.float32(2.0 * math.pi / period)


def bf(table):
    return np.asarray(table, np.float32).astype(jnp.bfloat16)


def bins(h):
    at = np.arange(h, MID + 1 - h)
    return at, (N2 - at if h else at)


def forward_tables():
    inner = np.arange(N2)
    outer = np.arange(N1)
    band = np.arange(1, KB + 1)
    a = angles(inner, inner, N2)
    dft = np.zeros((2 * ROWS, FOLD * STAGED), np.float32)
    column = inner % FOLD * STAGED + inner // FOLD
    dft[: MID + 1, column] = np.cos(a[: MID + 1])
    dft[ROWS : ROWS + MID + 1, column] = -np.sin(a[: MID + 1])
    t = angles(inner, outer, N1 * N2)
    twist = np.zeros((2, 2, ROWS, N1), np.float32)
    for h in range(2):
        at, k2 = bins(h)
        twist[h, 0, at] = np.cos(t[k2])
        twist[h, 1, at] = np.sin(t[k2])
    o = angles(outer, band, N1)
    c, s = np.cos(o), np.sin(o)
    last = np.stack([np.concatenate([c, -s, c, -s], 1), np.concatenate([s, c, s, c], 1)])
    return bf(dft), bf(twist), bf(last)


def backward_tables():
    inner = np.arange(N2)
    outer = np.arange(N1)
    band = np.arange(1, KB + 1)
    o = angles(band, outer, N1)
    c, s = np.cos(o), np.sin(o)
    back = np.zeros((4 * HALF, 4 * WIDE), np.float32)
    for h in range(2):
        row, col = h * HALF, 2 * h * WIDE
        re, im = slice(col, col + N1), slice(col + WIDE, col + WIDE + N1)
        for at, to_re, to_im in (
            (row, c, s),
            (row + KB, s, -c),
            (2 * HALF + row, -s, c),
            (2 * HALF + row + KB, c, s),
        ):
            back[at : at + KB, re] = to_re
            back[at : at + KB, im] = to_im
    t = angles(inner, outer, N1 * N2)
    twist = np.zeros((2, 2, ROWS, WIDE), np.float32)
    for h in range(2):
        at, k2 = bins(h)
        twist[h, 0, at, :N1] = np.cos(t[k2])
        twist[h, 1, at, :N1] = np.sin(t[k2])
    l = angles(np.arange(-H, H) % N2, inner, N2)
    lag = np.zeros((2, 2 * H, 2, ROWS), np.float32)
    at = np.arange(MID + 1)
    c, s = np.cos(l[:, at]), np.sin(l[:, at])
    lag[0, :, 0, at], lag[0, :, 1, at] = c.T, -s.T
    lag[1, :, 0, at], lag[1, :, 1, at] = c.T, s.T
    return bf(back), bf(twist), bf(lag.reshape(2, 2 * H, 2 * ROWS))


def spectrum_kernel(
    pick_hbm, x_hbm, dft_hbm, twist_hbm, last_hbm, out_ref, pick_ref, x_ref, stage, dft_ref, twist_ref, last_ref, sems
):
    copies = [
        pltpu.make_async_copy(source, target, sems.at[i])
        for i, (source, target) in enumerate(
            (
                (x_hbm, x_ref),
                (dft_hbm, dft_ref),
                (twist_hbm, twist_ref),
                (last_hbm, last_ref),
                (pick_hbm, pick_ref),
            )
        )
    ]
    for copy in copies:
        copy.start()
    tiles = STEP // 128
    copies[0].wait()
    stage[:, STAGED * STATIONS - 16 :] = jnp.zeros((tiles, 16, 128), jnp.float32)
    for a in range(FULL):
        chunk = x_ref[0, :, a * STEP : (a + 1) * STEP].astype(jnp.float32)
        for c in range(tiles):
            stage[c, a * STATIONS : (a + 1) * STATIONS] = chunk[:, c * 128 : (c + 1) * 128]
    rest = x_ref[0, :, FULL * STEP :].astype(jnp.float32)
    rest = jnp.concatenate([rest, jnp.zeros((STATIONS, STEP - rest.shape[1]), jnp.float32)], 1)
    for c in range(tiles):
        stage[c, FULL * STATIONS : (FULL + 1) * STATIONS] = rest[:, c * 128 : (c + 1) * 128]
    for copy in copies[1:]:
        copy.wait()
    turns = [[twist_ref[h, i].astype(jnp.float32) for i in range(2)] for h in range(2)]
    lane = lax.broadcasted_iota(jnp.int32, (ROWS, 2 * HALF), 1)
    reals, imags = [], []
    for t in range(STATIONS):
        at = pl.ds(t, STAGED, stride=STATIONS)
        rows = jnp.concatenate([stage.at[c][at] for c in range(tiles)], 1)
        v = jnp.concatenate([rows[:, r * N1 : (r + 1) * N1] for r in range(FOLD)], 0)
        y = jnp.dot(dft_ref[...], v.astype(jnp.bfloat16), preferred_element_type=jnp.float32)
        re, im = y[:ROWS], y[ROWS:]
        for (cosine, sine), conjugate in zip(turns, (im, -im)):
            reals.append((re * cosine + conjugate * sine).astype(jnp.bfloat16))
            imags.append((conjugate * cosine - re * sine).astype(jnp.bfloat16))
    spectra = jnp.dot(jnp.concatenate(reals, 0), last_ref[0], preferred_element_type=jnp.float32)
    spectra = spectra + jnp.dot(jnp.concatenate(imags, 0), last_ref[1], preferred_element_type=jnp.float32)
    row = lax.broadcasted_iota(jnp.int32, (8, 2 * HALF), 0)
    upper = lax.broadcasted_iota(jnp.int32, (8, 2 * HALF), 1) >= HALF
    spare = [(row == 0) & upper, (row == 6) & upper, (row == 7) & upper, (row == 7) & ~upper]
    for t in range(STATIONS):
        x = spectra[2 * ROWS * t : 2 * ROWS * (t + 1)]
        power = x * x
        size = jnp.sqrt(power + pltpu.roll(power, KB, 1))
        level = jnp.sum(size, axis=0, keepdims=True) * (1.0 / N2) + 1e-6
        w = x * (1.0 / level)
        packed = jnp.where(lane < HALF, w[:ROWS], w[ROWS:])
        for f in range(FAR):
            ends = [packed[:8], packed[ROWS - 8 :]]
            for i in range(NEAR // STATIONS):
                wanted = pick_ref[f * NEAR + t * (NEAR // STATIONS) + i].astype(jnp.float32)
                ends[i > 0] = jnp.where(spare[i], wanted, ends[i > 0])
            whole = jnp.concatenate([ends[0], packed[8 : ROWS - 8], ends[1]], 0)
            out_ref[f, t] = whole.astype(jnp.bfloat16)


def spectrum_call(pick, x):
    dft, twist, last = forward_tables()
    vmem = pl.BlockSpec(memory_space=pltpu.VMEM)
    hbm = pl.BlockSpec(memory_space=pl.ANY)
    return pl.pallas_call(
        spectrum_kernel,
        out_shape=pltpu.VMEM((FAR, STATIONS, ROWS, 2 * HALF), jnp.bfloat16),
        in_specs=[hbm, hbm, hbm, hbm, hbm],
        out_specs=vmem,
        scratch_shapes=[
            pltpu.SMEM(pick.shape, jnp.int32),
            pltpu.VMEM(x.shape, jnp.bfloat16),
            pltpu.VMEM((STEP // 128, STAGED * STATIONS, 128), jnp.float32),
            pltpu.VMEM(dft.shape, jnp.bfloat16),
            pltpu.VMEM(twist.shape, jnp.bfloat16),
            pltpu.VMEM(last.shape, jnp.bfloat16),
            pltpu.SemaphoreType.DMA((5,)),
        ],
        compiler_params=pltpu.CompilerParams(vmem_limit_bytes=56 * 2**20),
        name="spectrum",
    )(pick, x, jnp.asarray(dft), jnp.asarray(twist), jnp.asarray(last))


def choose_kernel(x_ref, out_ref):
    lane = lax.broadcasted_iota(jnp.int32, (8, 2 * HALF), 1)
    for f in range(FAR):
        wanted = []
        for t in range(STATIONS):
            head = x_ref[f, t, :16].astype(jnp.float32)[:8]
            tail = x_ref[f, t, ROWS - 8 :].astype(jnp.float32)
            head = jnp.where(lane < HALF, pltpu.roll(head, HALF, 1), head)
            turned = pltpu.roll(tail, HALF, 1)
            upper = jnp.where(lane < HALF, turned, tail)
            lower = jnp.where(lane < HALF, tail, turned)
            for line in (head[:1], upper[6:7], upper[7:], lower[7:]):
                wanted.append(jnp.broadcast_to(line, (16, 2 * HALF)).astype(jnp.bfloat16))
        for k in range(0, ROWS, 16):
            n = min(16, ROWS - k)
            parts = [x_ref[f, t, k : k + n] for t in range(STATIONS)]
            for d in range(NEAR):
                best = parts[0]
                for t in range(1, STATIONS):
                    best = jnp.where(wanted[d][:n] == t, parts[t], best)
                out_ref[d, f, k : k + n] = best


def choose_call(x):
    vmem = pl.BlockSpec(memory_space=pltpu.VMEM)
    return pl.pallas_call(
        choose_kernel,
        out_shape=jax.ShapeDtypeStruct((NEAR, FAR, ROWS, 2 * HALF), jnp.bfloat16),
        in_specs=[vmem],
        out_specs=vmem,
        compiler_params=pltpu.CompilerParams(vmem_limit_bytes=48 * 2**20),
        name="choose",
    )(x)


def place(owner):
    return (owner & (NEAR - 1)) * FAR + (owner >> 4)


def lag_kernel(row_ref, w_ref, back_ref, twist_ref, lag_ref, out_ref, stage, product):
    lane = lax.broadcasted_iota(jnp.int32, (ROWS, 2 * HALF), 1) % HALF
    s = w_ref[place(row_ref[0])].astype(jnp.float32)
    s1 = jnp.where(lane < KB, s, pltpu.roll(s, KB, 1)).astype(jnp.bfloat16)
    s2 = jnp.where(lane < KB, pltpu.roll(s, 2 * HALF - KB, 1), s).astype(jnp.bfloat16)
    scale = 1.0 / math.sqrt(KB * N2)

    for i in range(PAIRS):
        r = w_ref[place(row_ref[i + 1])]
        product[i, :ROWS] = jnp.concatenate([r * s1, r * s2], 1)
    both = product[...].reshape(PAIRS * PITCH, 4 * HALF)
    turned = [[] for _ in range(PAIRS)]
    for h in range(2):
        z = jnp.dot(
            both,
            back_ref[:, 2 * h * WIDE : 2 * (h + 1) * WIDE],
            preferred_element_type=jnp.float32,
        ).astype(jnp.bfloat16)
        cosine, sine = twist_ref[h, 0], twist_ref[h, 1]
        for i in range(PAIRS):
            mine = z[i * PITCH : i * PITCH + ROWS]
            re, im = mine[:, :WIDE], mine[:, WIDE:]
            a = re * cosine - im * sine
            b = re * sine + im * cosine
            turned[i].append((a, b))
    for i in range(PAIRS):
        (a0, b0), (a1, b1) = turned[i]
        sides = (a0 + a1, b0 - b1), (b0 + b1, a0 - a1)
        re, im = (
            jnp.dot(lag_ref[k], jnp.concatenate(side, 0), preferred_element_type=jnp.float32) * scale
            for k, side in enumerate(sides)
        )
        at = pl.ds(i * 2 * H, 2 * H)
        for lanes in range(2):
            stage[lanes, at] = re[:, lanes * 128 : (lanes + 1) * 128]
            stage[2 + lanes, at] = im[:, lanes * 128 : (lanes + 1) * 128]

    for j in range(H):
        rows = [
            stage.at[lanes][pl.ds(2 * j + n, PAIRS, stride=2 * H)]
            for lanes in range(4)
            for n in range(2)
        ]
        out_ref[j] = jnp.concatenate(rows, 0).astype(jnp.bfloat16)


def lag_call(rows, w):
    back, twist, lag = backward_tables()
    vmem = pl.BlockSpec(memory_space=pltpu.VMEM)
    return pl.pallas_call(
        lag_kernel,
        out_shape=jax.ShapeDtypeStruct((H, LAGROWS, 128), jnp.bfloat16),
        in_specs=[pl.BlockSpec(memory_space=pltpu.SMEM), vmem, vmem, vmem, vmem],
        out_specs=vmem,
        scratch_shapes=[
            pltpu.VMEM((4, PAIRS * 2 * H, 128), jnp.float32),
            pltpu.VMEM((PAIRS, PITCH, 4 * HALF), jnp.bfloat16),
        ],
        compiler_params=pltpu.CompilerParams(vmem_limit_bytes=48 * 2**20),
        name="lags",
    )(rows, w, jnp.asarray(back), jnp.asarray(twist), jnp.asarray(lag))


def stack_kernel(x_ref, out_ref):
    segments = x_ref.shape[0]
    half = LAGROWS // 2
    linear = phase_re = phase_im = None
    for s in range(segments):
        x = x_ref[s].astype(jnp.float32)
        re, im = x[:half], x[half:]
        inverse = jnp.minimum(lax.rsqrt(re * re + im * im), 4.0)
        if s == 0:
            linear, phase_re, phase_im = re, re * inverse, im * inverse
        else:
            linear = linear + re
            phase_re = phase_re + re * inverse
            phase_im = phase_im + im * inverse
    coherence = jnp.sqrt(phase_re * phase_re + phase_im * phase_im)
    pws = linear * coherence * (1.0 / segments)
    for n in range(2):
        low = pws[n * PAIRS : (n + 1) * PAIRS]
        high = pws[(2 + n) * PAIRS : (3 + n) * PAIRS]
        out_ref[:, n * N1 : (n + 1) * N1] = jnp.concatenate([low, high], 1)[:, :N1]


def stack_call(x):
    vmem = pl.BlockSpec(memory_space=pltpu.VMEM)
    return pl.pallas_call(
        stack_kernel,
        out_shape=jax.ShapeDtypeStruct((PAIRS, 2 * N1), jnp.float32),
        in_specs=[vmem],
        out_specs=vmem,
        compiler_params=pltpu.CompilerParams(vmem_limit_bytes=48 * 2**20),
        name="stack",
    )(x)


def local(traces, block_sources, send_lists):
    pick = send_lists.reshape(-1)
    rows = block_sources.reshape(-1)
    whitened = spectrum_call(pick, traces)
    whitened = lax.all_to_all(whitened, "far", split_axis=0, concat_axis=0, tiled=True)
    chosen = choose_call(whitened)
    chosen = lax.all_to_all(chosen, ("near", "cell"), split_axis=0, concat_axis=0, tiled=True)
    lags = lag_call(rows, chosen.reshape(FAR * NEAR, ROWS, 2 * HALF))
    lags = lax.all_to_all(lags, "seg", split_axis=0, concat_axis=0, tiled=True)
    return stack_call(lags)


def solution(mesh):
    split = Mesh(mesh.devices.reshape(FAR, 2, NEAR // 2, -1), ("far", "near", "cell", "seg"))
    pairs = ("far", "near", "cell")
    return jax.shard_map(
        local,
        mesh=split,
        in_specs=(P("seg", pairs, None), P(pairs, None), P(pairs, None, None)),
        out_specs=P(pairs, "seg"),
        check_vma=False,
    )
```
